32 devices in a mesh: section: 2 (over y), inst: 2 (over x), tensor: 8 (over z, core).
Axes of the slice: x: 2, y: 2, z: 4, core: 2. Of those that a mesh axis runs over, the one named last changes fastest.
Arguments:
- hidden_in: bfloat16 [64, 8192], P('inst', 'tensor'), may hold values from -3 to 3
- queries: bfloat16 [2, 64, 8192], P('section', 'inst', 'tensor'), may hold values from -24 to 24
- new_kv: bfloat16 [2, 64, 2048], P('section', 'inst'), may hold values from -8 to 8
- kv_pages: bfloat16 [2, 16, 256, 2048], P('section', 'inst', 'tensor'), may hold values from -8 to 8
- out_weight: bfloat16 [2, 8192, 8192], P('section', 'tensor'), may hold values from -0.09375 to 0.09375
- move_pages: int32 [2, 2, 1], P('inst'), may hold values from 0 to 7, as said below
- page_table: int32 [16, 4], P('inst'), may hold values from 0 to 9, as said below
- lengths: int32 [16], P('inst'), may hold values from 256 to 1024, as said below
Outputs:
- residual: bfloat16 [2, 64, 8192], P('section', 'inst', 'tensor')
The draws below stay inside these ranges and needn't reach their ends.
Inputs may be any that keep to these rules, and one draw needn't show every extreme that they name: `move_pages`: source page ids of the move; pages may repeat. `page_table`: pages may be shared between requests of one instance; the first page of every request is one received in the move, from source instance r % 8 % 2. `lengths`: every request has at least one full page.
All inputs are finite; a program needn't handle non-finite values.
Results may differ from the reference program's by a relative error of at most 0.015.
Values may be sent and summed in bfloat16 or wider, within the bound.
No kernel may reach another device: no remote copies, remote signals or barrier semaphores. Data moves between devices by JAX's collectives and lax.ppermute only.
A program may use at most 128 MiB of HBM per device.

```python
import jax
import jax.numpy as jnp
from jax import lax

D = 8192
HEADS = 64
KVH = 8
HD = 128
PAGE = 256
STEPS = 4
MAXP = 4
NPAGES = 8
CAP = 1
RI = 8
MAXLEN = 1024
LOCAL = 10
ROWS = 64
LAYERS = 2
N_SECTION = 2
N_INST = 2


def draw_queries(key, part):
    key = jax.random.fold_in(key, 1)
    shape = (N_SECTION, N_INST * RI * STEPS, KVH, HEADS // KVH, HD)
    noise_values = jax.random.normal(key, shape, jnp.float32)
    noise_values = jnp.clip(noise_values, -24.0, 24.0)
    return noise_values.reshape(N_SECTION, N_INST * RI * STEPS, HEADS * HD).astype(jnp.bfloat16)


def lifted_tokens(key, shape):
    noise_values = jax.random.normal(key, shape, jnp.float32)
    return jnp.clip(noise_values, -8.0, 8.0)


def draw_new_kv(key, part):
    key = jax.random.fold_in(key, 2)
    tokens = lifted_tokens(key, (N_SECTION, N_INST * RI * STEPS, KVH, 2, HD))
    return tokens.reshape(N_SECTION, N_INST * RI * STEPS, KVH * 2 * HD).astype(jnp.bfloat16)


def draw_kv_pages(key, part):
    key = jax.random.fold_in(key, 3)
    tokens = lifted_tokens(key, (N_SECTION, N_INST * NPAGES, PAGE, KVH, 2, HD))
    return tokens.reshape(N_SECTION, N_INST * NPAGES, PAGE, KVH * 2 * HD).astype(jnp.bfloat16)


def draw_move_pages(key, part):
    key = jax.random.fold_in(key, 13)
    chosen = jax.random.randint(key, (N_INST, N_INST, CAP), 0, NPAGES)
    chosen = chosen.at[0, 0, 0].set(0)
    chosen = chosen.at[1, N_INST - 1, CAP - 1].set(NPAGES - 1)
    return chosen.astype(jnp.int32)


def draw_page_table(key, part):
    key = jax.random.fold_in(key, 12)
    page_choice = jax.random.randint(key, (N_INST * RI, MAXP), 0, LOCAL)
    local_slot = jnp.arange(N_INST * RI, dtype=jnp.int32) % RI
    page_choice = page_choice.at[:, 0].set(NPAGES + local_slot % (N_INST * CAP))
    page_choice = page_choice.at[:, 1].set(jnp.where(local_slot == 0, 0, page_choice[:, 1]))
    return page_choice.astype(jnp.int32)


def draw_lengths(key, part):
    key = jax.random.fold_in(key, 11)
    length_values = jax.random.randint(key, (N_INST * RI,), PAGE, MAXLEN + 1)
    spot_key = jax.random.fold_in(key, 2)
    chosen_spot = jax.random.randint(spot_key, (), 0, N_INST * RI)
    length_values = length_values.at[chosen_spot].set(MAXLEN)
    length_values = length_values.at[(chosen_spot + 1) % (N_INST * RI)].set(PAGE)
    return length_values.astype(jnp.int32)


def with_spikes(result, own_key, source, target, parts, factor):
    def block_of(dim):
        return (jnp.arange(result.shape[dim]) // (result.shape[dim] // parts)).reshape((-1,) + (1,) * (result.ndim - 1 - dim))

    near = jax.random.permutation(own_key, parts)[block_of(target)]
    other_side = (block_of(target) + parts // 2) % parts
    return jnp.where((block_of(source) == near) | (block_of(source) == other_side), factor * result, result)


def shard_levels(key, dims, shards, smallest, top_value):
    gain, own = 1.0, jax.random.fold_in(key, 6)
    for axis_at, shards_of in shards:
        steps = jnp.exp(jax.random.uniform(jax.random.fold_in(own, axis_at), (shards_of,), jnp.float32, smallest / len(shards), top_value / len(shards)))
        gain = gain * jnp.repeat(steps, dims[axis_at] // shards_of).reshape([-1 if axis == axis_at else 1 for axis in range(len(dims))])
    return gain


def bell_draw(own_key, shape, scale, most, split=(), kind=jnp.bfloat16):
    values = jax.random.normal(own_key, shape, jnp.float32) * scale
    if len(split) > 0:
        values = shard_levels(own_key, shape, split, -0.22, 0.18) * values
    return jnp.clip(values, min=-most, max=most).astype(kind)


def heavy_noise(own_key, extent, scale, most, split, heavy, held_as=jnp.bfloat16):
    values = scale * jax.random.normal(own_key, extent, jnp.float32)
    if split:
        values = values * shard_levels(own_key, extent, split, -0.22, 0.18)
    return jnp.clip(with_spikes(values, jax.random.fold_in(own_key, 3), *heavy), -most, most).astype(held_as)


def setup_inputs(seed: int = 0) -> dict:
    splits = jax.random.split(jax.random.key(seed), 9)
    hidden_in = bell_draw(splits[0], (ROWS, D), 0.5, 3.0, ((0, 2), (1, 8)))
    queries = draw_queries(jax.random.fold_in(splits[8], 71), 0)
    new_kv = draw_new_kv(jax.random.fold_in(splits[8], 71), 0)
    kv_pages = draw_kv_pages(jax.random.fold_in(splits[8], 71), 0)
    out_weight = heavy_noise(splits[4], (LAYERS, HEADS * HD, D), (HEADS * HD) ** -0.5, 0.09375, ((0, 2), (1, 8)), (1, 2, 8, 2.0))
    move_pages = draw_move_pages(jax.random.fold_in(splits[8], 71), 0)
    page_table = draw_page_table(jax.random.fold_in(splits[8], 71), 0)
    lengths = draw_lengths(jax.random.fold_in(splits[8], 71), 0)
    return dict(hidden_in=hidden_in, queries=queries, new_kv=new_kv, kv_pages=kv_pages, out_weight=out_weight, move_pages=move_pages, page_table=page_table, lengths=lengths)


def reference(hidden_in, queries, new_kv, kv_pages, out_weight, move_pages, page_table, lengths):
    group_size = HEADS // KVH
    score_scale = 1.0 / (HD ** 0.5)
    width = KVH * 2 * HD
    current = hidden_in
    results = []
    for layer_index in range(N_SECTION):
        own_pages = kv_pages[layer_index].reshape(N_INST, NPAGES, PAGE, width)
        sources = jnp.arange(N_INST, dtype=jnp.int32)
        arrived = own_pages[sources[:, None, None], move_pages]
        arrived = jnp.transpose(arrived, (1, 0, 2, 3, 4)).reshape(N_INST, N_INST * CAP, PAGE, width)
        page_pool = jnp.concatenate([own_pages, arrived], axis=1)
        layer_queries = queries[layer_index]
        layer_new = new_kv[layer_index]

        def attend_request(request):
            instance = request // RI
            chosen = page_pool[instance][page_table[request]]
            cached_tokens = chosen.reshape(MAXP * PAGE, KVH, 2 * HD)
            fresh_tokens = lax.dynamic_slice_in_dim(layer_new, request * STEPS, STEPS, 0).reshape(STEPS, KVH, 2 * HD)
            all_tokens = jnp.concatenate([cached_tokens, fresh_tokens], axis=0).astype(jnp.float32)
            key_part = all_tokens[:, :, :HD]
            value_part = all_tokens[:, :, HD:]
            row_queries = lax.dynamic_slice_in_dim(layer_queries, request * STEPS, STEPS, 0)
            row_queries = row_queries.reshape(STEPS, KVH, group_size, HD).astype(jnp.float32)
            scores = jnp.einsum('sgqd,tgd->sgqt', row_queries, key_part) * score_scale
            cached_live = jnp.arange(MAXP * PAGE, dtype=jnp.int32) < lengths[request]
            step_ids = jnp.arange(STEPS, dtype=jnp.int32)
            fresh_live = step_ids[None, :] <= step_ids[:, None]
            live_mask = jnp.concatenate([jnp.broadcast_to(cached_live[None, :], (STEPS, MAXP * PAGE)), fresh_live], axis=1)
            live_mask = live_mask[:, None, None, :]
            scores = jnp.where(live_mask, scores, jnp.float32(-1e30))
            row_max = jnp.max(scores, axis=-1, keepdims=True)
            expo = jnp.where(live_mask, jnp.exp(scores - row_max), jnp.float32(0.0))
            weight_sum = jnp.sum(expo, axis=-1)
            weights = lax.optimization_barrier(expo.astype(jnp.bfloat16)).astype(jnp.float32)
            weighted = jnp.einsum('sgqt,tgd->sgqd', weights, value_part)
            attended = (weighted / weight_sum[..., None]).astype(jnp.bfloat16)
            return attended.reshape(STEPS, HEADS * HD)

        attended_all = lax.map(attend_request, jnp.arange(N_INST * RI, dtype=jnp.int32))
        attended_all = attended_all.reshape(N_INST * RI * STEPS, HEADS * HD)
        projected = jnp.dot(attended_all, out_weight[layer_index], preferred_element_type=jnp.float32)
        current = (current.astype(jnp.float32) + projected).astype(jnp.bfloat16)
        results.append(current)
    return jnp.stack(results, axis=0)
```

```python
import functools
import math

import jax
import jax.numpy as jnp
from jax import lax
from jax.experimental import pallas as pl
from jax.experimental.pallas import tpu as pltpu
from jax.sharding import PartitionSpec as P

HEADS = 64
KVH = 8
HD = 128
STEPS = 4
GROUP = HEADS // KVH
MASKED = -1e30
LOG2E = 1.4426950408889634


def swapped(value, mask):
    count = lax.axis_size("tensor")
    return lax.ppermute(value, "tensor", [(source, source ^ mask) for source in range(count)])


def attend_kernel(
    requests, page_tokens, pages, tensor_count, inst_count, capacity, query_count, piece_count, *refs
):
    place, table, lengths, moves = refs[:4]
    queries = refs[4 : 4 + query_count]
    pieces = refs[4 + query_count : 4 + query_count + piece_count]
    outputs = refs[4 + query_count + piece_count :]
    tensor_rank, inst_rank = place[0], place[1]
    per = max(1, tensor_count // KVH)
    head_rank = tensor_rank // per
    partner = tensor_rank ^ per
    rows = requests * STEPS
    slots = table.shape[1]
    page_size = page_tokens * tensor_count

    row = lax.broadcasted_iota(jnp.int32, (rows, 1), 0)
    row_request, row_step = row // STEPS, row % STEPS
    row_length = jnp.zeros((rows, 1), jnp.int32)
    row_pages = [jnp.zeros((rows, 1), jnp.int32) for _ in range(slots)]
    for request in range(requests):
        here = row_request == request
        row_length = jnp.where(here, lengths[request], row_length)
        for slot in range(slots):
            page = table[request, slot]
            arrived = page - pages
            for own in range(capacity):
                page = jnp.where(arrived == inst_rank * capacity + own, moves[inst_rank, own], page)
            row_pages[slot] = jnp.where(here, page, row_pages[slot])

    def times_used(page, token):
        used = jnp.zeros((rows, page.shape[1]), jnp.float32)
        for slot in range(slots):
            live = (row_pages[slot] == page) & (token + slot * page_size < row_length)
            used = used + jnp.where(live, 1.0, 0.0)
        return used

    def column(count):
        return lax.broadcasted_iota(jnp.int32, (1, count), 1)

    def arrived_page(block):
        shift = block // capacity + 1
        source = inst_rank - shift
        source = jnp.where(source < 0, source + inst_count, source)
        return pages + source * capacity + block % capacity

    use = []
    own_columns = pages * page_tokens
    moved_columns = (inst_count - 1) * capacity * page_tokens
    for rank in (tensor_rank, partner):
        spot = column(own_columns)
        use.append(times_used(spot // page_tokens, rank * page_tokens + spot % page_tokens))
    for rank in (tensor_rank, partner):
        spot = column(moved_columns)
        use.append(
            times_used(arrived_page(spot // page_tokens), rank * page_tokens + spot % page_tokens)
        )
    spot = column(rows)
    fresh = (spot // STEPS == row_request) & (spot % STEPS <= row_step)
    fresh = fresh & ((tensor_rank == 0) | (tensor_rank == per))
    use.append(jnp.where(fresh, 1.0, 0.0))
    use = jnp.concatenate(use, axis=1)
    columns = use.shape[1]
    use = use[None]

    heads_per = HEADS // tensor_count
    lane = lax.broadcasted_iota(jnp.int32, (rows, HD), 1)
    factor = LOG2E / math.sqrt(HD)
    for group in range(query_count // per):
        kv_head = head_rank ^ (2 * group)
        base = pl.multiple_of(kv_head * (2 * HD), 2 * HD)
        keys = jnp.concatenate([piece[:, pl.ds(base, HD)] for piece in pieces], axis=0)
        values = jnp.concatenate(
            [piece[:, pl.ds(pl.multiple_of(base + HD, HD), HD)] for piece in pieces], axis=0
        )
        blocks = []
        for low in range(per):
            block = queries[group * per + low]
            blocks += [block[:, head * HD : (head + 1) * HD] for head in range(heads_per)]
        stacked = jnp.concatenate(blocks, axis=0)
        scores = lax.dot_general(
            stacked, keys, (((1,), (1,)), ((), ())), preferred_element_type=jnp.float32
        )
        scores = scores.reshape(GROUP, rows, columns)
        scores = jnp.where(use > 0.0, scores, MASKED)
        row_max = jnp.max(scores, axis=-1, keepdims=True)
        expo = jnp.exp2((scores - row_max) * factor) * use
        total = jnp.sum(expo, axis=-1, keepdims=True)
        weighted = jnp.dot(
            expo.astype(jnp.bfloat16).reshape(GROUP * rows, columns),
            values,
            preferred_element_type=jnp.float32,
        )
        weighted = (weighted.reshape(GROUP, rows, HD) / total).astype(jnp.bfloat16)
        level = row_max * factor + jnp.log2(total)
        for low in range(per):
            out = outputs[group * per + low]
            stat = jnp.zeros((rows, HD), jnp.float32)
            for head in range(heads_per):
                at = low * heads_per + head
                out[:, head * HD : (head + 1) * HD] = weighted[at]
                stat = jnp.where(lane % heads_per == head, level[at], stat)
            top = stat.astype(jnp.bfloat16).astype(jnp.float32)
            rest = stat - top
            middle = rest.astype(jnp.bfloat16).astype(jnp.float32)
            stat = jnp.where(
                lane < heads_per, top, jnp.where(lane < 2 * heads_per, middle, rest - middle)
            )
            out[:, heads_per * HD :] = stat.astype(jnp.bfloat16)


def combine(parts, heads_per):
    levels = []
    for part in parts:
        stat = part[:, heads_per * HD :].astype(jnp.float32)
        levels.append(
            stat
            + pltpu.roll(stat, HD - heads_per, 1)
            + pltpu.roll(stat, HD - 2 * heads_per, 1)
        )
    top = functools.reduce(jnp.maximum, levels)
    shares = [jnp.exp2(level - top) for level in levels]
    total = sum(shares[1:], shares[0])
    shares = [share / total for share in shares]
    heads = []
    for head in range(heads_per):
        terms = [
            share[:, head : head + 1] * part[:, head * HD : (head + 1) * HD].astype(jnp.float32)
            for share, part in zip(shares, parts)
        ]
        heads.append(sum(terms[1:], terms[0]).astype(jnp.bfloat16))
    return jnp.concatenate(heads, axis=1)


def first_project_kernel(heads_per, part_count, place, *refs):
    parts, (weight, out, attended) = refs[:part_count], refs[part_count:]

    @pl.when(pl.program_id(0) == 0)
    def _():
        attended[...] = combine(parts, heads_per)

    out[0] = jnp.dot(
        attended[...], weight[0], preferred_element_type=jnp.float32
    ).astype(jnp.bfloat16)


def second_project_kernel(place, attended, other, weight, out, own):
    total = jnp.dot(attended[...], weight[0], preferred_element_type=jnp.float32)
    total = total + other[0].astype(jnp.float32)
    out[0] = total.astype(jnp.bfloat16)

    @pl.when(pl.program_id(0) == 0)
    def _():
        own[...] = total


def local(hidden_in, queries, new_kv, kv_pages, out_weight, move_pages, page_table, lengths):
    tensor_count = lax.axis_size("tensor")
    inst_count = lax.axis_size("inst")
    tensor_rank = lax.axis_index("tensor")
    inst_rank = lax.axis_index("inst")
    section_rank = lax.axis_index("section")
    per = max(1, tensor_count // KVH)
    heads_per = HEADS // tensor_count
    requests = page_table.shape[0]
    rows = requests * STEPS
    own_pages = kv_pages[0]
    pages, page_tokens, width = own_pages.shape
    capacity = move_pages.shape[2]
    moves = move_pages[0]
    peers = [mask for mask in range(tensor_count) if mask & per == 0]

    own_queries = queries[0]
    all_queries = [own_queries] + [swapped(own_queries, mask) for mask in peers[1:]]
    own_flat = own_pages.reshape(pages * page_tokens, width)
    partner_flat = swapped(own_flat, per)
    arrived = []
    for shift in range(1, inst_count):
        leaving = own_pages[moves[(inst_rank + shift) % inst_count]]
        pairs = [(source, (source + shift) % inst_count) for source in range(inst_count)]
        arrived.append(lax.ppermute(leaving.reshape(-1, width), "inst", pairs))
    arrived = arrived[0] if len(arrived) == 1 else jnp.concatenate(arrived, axis=0)
    partner_arrived = swapped(arrived, per)
    pieces = [own_flat, partner_flat, arrived, partner_arrived, new_kv[0]]
    if arrived.shape[0] % 16:
        pieces = pieces[:2] + [jnp.concatenate([arrived, partner_arrived], axis=0)] + pieces[4:]

    place = jnp.stack([tensor_rank, inst_rank]).astype(jnp.int32)
    smem = pl.BlockSpec(memory_space=pltpu.SMEM)
    vmem = pl.BlockSpec(memory_space=pltpu.VMEM)
    part_shape = jax.ShapeDtypeStruct((rows, heads_per * HD + HD), jnp.bfloat16)
    parts = pl.pallas_call(
        functools.partial(
            attend_kernel,
            requests,
            page_tokens,
            pages,
            tensor_count,
            inst_count,
            capacity,
            len(peers),
            len(pieces),
        ),
        out_shape=[part_shape] * len(peers),
        in_specs=[smem] * 4 + [vmem] * (len(peers) + len(pieces)),
        out_specs=[vmem] * len(peers),
        compiler_params=pltpu.CompilerParams(vmem_limit_bytes=32 * 1024 * 1024),
        name="attend",
    )(place, page_table, lengths, moves, *all_queries, *pieces)
    parts = [parts[0]] + [swapped(part, mask) for part, mask in zip(parts[1:], peers[1:])]

    depth, features = out_weight.shape[1:]
    chunk = features // tensor_count
    half = tensor_count // 2
    part_spec = pl.BlockSpec(part_shape.shape, lambda step, place: (0, 0))
    attended_spec = pl.BlockSpec((rows, depth), lambda step, place: (0, 0))
    chunk_spec = pl.BlockSpec((1, rows, chunk), lambda step, place: (step, 0, 0))
    away, attended = pl.pallas_call(
        functools.partial(first_project_kernel, heads_per, len(peers)),
        grid_spec=pltpu.PrefetchScalarGridSpec(
            num_scalar_prefetch=1,
            grid=(half,),
            in_specs=[part_spec] * len(peers)
            + [pl.BlockSpec((1, depth, chunk), lambda step, place: (0, 0, place[0] ^ (2 * step + 1)))],
            out_specs=[chunk_spec, attended_spec],
        ),
        out_shape=[
            jax.ShapeDtypeStruct((half, rows, chunk), jnp.bfloat16),
            jax.ShapeDtypeStruct((rows, depth), jnp.bfloat16),
        ],
        compiler_params=pltpu.CompilerParams(vmem_limit_bytes=32 * 1024 * 1024),
        name="project_away",
    )(place, *parts, out_weight)
    other = swapped(away, 1)
    paired, own = pl.pallas_call(
        second_project_kernel,
        grid_spec=pltpu.PrefetchScalarGridSpec(
            num_scalar_prefetch=1,
            grid=(half,),
            in_specs=[
                attended_spec,
                chunk_spec,
                pl.BlockSpec((1, depth, chunk), lambda step, place: (0, 0, place[0] ^ (2 * step))),
            ],
            out_specs=[chunk_spec, pl.BlockSpec((rows, chunk), lambda step, place: (0, 0))],
        ),
        out_shape=[
            jax.ShapeDtypeStruct((half, rows, chunk), jnp.bfloat16),
            jax.ShapeDtypeStruct((rows, chunk), jnp.float32),
        ],
        compiler_params=pltpu.CompilerParams(vmem_limit_bytes=32 * 1024 * 1024),
        name="project_home",
    )(place, attended, other, out_weight)
    projected = own
    for at in range(1, half):
        projected = projected + swapped(paired[at], 2 * at).astype(jnp.float32)
    after_first = (hidden_in.astype(jnp.float32) + projected).astype(jnp.bfloat16)
    handed_over = lax.ppermute(after_first, "section", [(0, 1), (1, 0)])
    after_second = (handed_over.astype(jnp.float32) + projected).astype(jnp.bfloat16)
    result = jnp.where(section_rank == 0, after_first, after_second)
    return result[None]


def solution(mesh):
    return jax.shard_map(
        local,
        mesh=mesh,
        in_specs=(
            P("inst", "tensor"),
            P("section", "inst", "tensor"),
            P("section", "inst", None),
            P("section", "inst", "tensor", None),
            P("section", "tensor", None),
            P("inst", None, None),
            P("inst", None),
            P("inst"),
        ),
        out_specs=P("section", "inst", "tensor"),
        check_vma=False,
    )
```

```python
import functools
import math

import jax
import jax.numpy as jnp
from jax import lax
from jax.experimental import pallas as pl
from jax.experimental.pallas import tpu as pltpu
from jax.sharding import PartitionSpec as P

HEADS = 64
KVH = 8
HD = 128
STEPS = 4
GROUP = HEADS // KVH
MASKED = -1e30
LOG2E = 1.4426950408889634
MEGA = 1024 * 1024


def swapped(value, mask):
    count = lax.axis_size("tensor")
    return lax.ppermute(value, "tensor", [(source, source ^ mask) for source in range(count)])


def in_hbm(value):
    return pltpu.with_memory_space_constraint(value, pltpu.HBM)


def weight_copies(weight, out, semaphores, masks):
    rank = lax.axis_index("tensor")
    chunk = out.shape[2]
    copies = []
    for at, mask in enumerate(masks):
        start = pl.multiple_of((rank ^ mask) * chunk, chunk)
        copies.append(
            pltpu.make_async_copy(
                weight.at[0, :, pl.ds(start, chunk)], out.at[at], semaphores.at[at]
            )
        )
    return copies


def pick_kernel(capacity, moves_hbm, pages, *refs):
    outputs, (moves, moves_semaphore, semaphores) = refs[:-3], refs[-3:]
    moves_copy = pltpu.make_async_copy(moves_hbm, moves, moves_semaphore)
    moves_copy.start()
    moves_copy.wait()
    tensor_count, inst_count = lax.axis_size("tensor"), lax.axis_size("inst")
    per = max(1, tensor_count // KVH)
    side = lax.axis_index("tensor") // per % 2
    copies = []
    for shift in range(1, inst_count):
        target = lax.axis_index("inst") + shift
        target = jnp.where(target >= inst_count, target - inst_count, target)
        for slot in range(capacity):
            page = moves[target * capacity + slot]
            for other in range(2):
                out = outputs[2 * (shift - 1) + other]
                for pair in range(KVH // 2):
                    head = 2 * pair + (side if other == 0 else 1 - side)
                    start = pl.multiple_of(head * (2 * HD), 2 * HD)
                    copies.append(
                        pltpu.make_async_copy(
                            pages.at[page, :, pl.ds(start, 2 * HD)],
                            out.at[slot, :, 2 * HD * pair : 2 * HD * (pair + 1)],
                            semaphores.at[len(copies)],
                        )
                    )
    for copy in copies:
        copy.start()
    for copy in copies:
        copy.wait()


def packed_level(level, lane, heads_per):
    top = level.astype(jnp.bfloat16).astype(jnp.float32)
    rest = level - top
    middle = rest.astype(jnp.bfloat16).astype(jnp.float32)
    level = jnp.where(lane < heads_per, top, jnp.where(lane < 2 * heads_per, middle, rest - middle))
    return level.astype(jnp.bfloat16)


def count_kernel(shape, weight_masks, table_hbm, lengths_hbm, moves_hbm, weight, *refs):
    use_out, weight_out, table, lengths, moves, semaphores, weight_semaphores = refs
    pages, page_tokens, capacity = shape
    tensor_count, inst_count = lax.axis_size("tensor"), lax.axis_size("inst")
    tensor_rank, inst_rank = lax.axis_index("tensor"), lax.axis_index("inst")
    per = max(1, tensor_count // KVH)
    partner = tensor_rank ^ per
    rows, columns = use_out.shape
    slots, requests = table.shape
    page_size = page_tokens * tensor_count
    copies = [
        pltpu.make_async_copy(source, target, semaphores.at[at])
        for at, (source, target) in enumerate(
            ((table_hbm, table), (lengths_hbm, lengths), (moves_hbm, moves))
        )
    ]
    load_copies = weight_copies(weight, weight_out, weight_semaphores, weight_masks)
    for copy in copies + load_copies:
        copy.start()
    for copy in copies:
        copy.wait()

    row = lax.broadcasted_iota(jnp.int32, (rows, 1), 0)
    row_request, row_step = row // STEPS, row % STEPS
    row_length = jnp.zeros((rows, 1), jnp.int32)
    row_pages = [jnp.zeros((rows, 1), jnp.int32) for _ in range(slots)]
    for request in range(requests):
        here = row_request == request
        row_length = jnp.where(here, lengths[request], row_length)
        for slot in range(slots):
            page = table[slot, request]
            arrived = page - pages
            for own in range(capacity):
                page = jnp.where(
                    arrived == inst_rank * capacity + own, moves[inst_rank * capacity + own], page
                )
            row_pages[slot] = jnp.where(here, page, row_pages[slot])

    column = lax.broadcasted_iota(jnp.int32, (1, columns), 1)
    own_columns = pages * page_tokens
    block_columns = capacity * page_tokens
    moved = column - 2 * own_columns
    block = moved // block_columns
    source = inst_rank - block // 2 - 1
    source = jnp.where(source < 0, source + inst_count, source)
    resident = moved < 0
    page = jnp.where(
        resident,
        column % own_columns // page_tokens,
        pages + source * capacity + moved // page_tokens % capacity,
    )
    side = jnp.where(resident, column // own_columns, block % 2)
    token = jnp.where(side == 0, tensor_rank, partner) * page_tokens + column % page_tokens
    use = jnp.zeros((rows, columns), jnp.float32)
    for slot in range(slots):
        live = (row_pages[slot] == page) & (token + slot * page_size < row_length)
        use = use + jnp.where(live, 1.0, 0.0)
    fresh = column - (columns - rows)
    fresh_live = (fresh // STEPS == row_request) & (fresh % STEPS <= row_step)
    fresh_live = fresh_live & ((tensor_rank == 0) | (tensor_rank == per))
    use_out[...] = jnp.where(fresh >= 0, jnp.where(fresh_live, 1.0, 0.0), use)
    for copy in load_copies:
        copy.wait()


def attend_kernel(masks, weight_masks, piece_count, *refs):
    tensor_count, tensor_rank = lax.axis_size("tensor"), lax.axis_index("tensor")
    use_ref, refs = refs[0], refs[1:]
    queries, refs = refs[: len(masks)], refs[len(masks) :]
    pieces, weight, refs = refs[:piece_count], refs[piece_count], refs[piece_count + 1 :]
    parts, refs = refs[: len(masks)], refs[len(masks) :]
    weight_out, own_queries, tokens, query_semaphore, semaphores, weight_semaphores = refs
    per = max(1, tensor_count // KVH)
    rows, columns = use_ref.shape
    heads_per = HEADS // tensor_count
    groups = len(masks) // per

    copies = []
    for group in range(groups):
        kv_head = (tensor_rank ^ masks[group * per]) // per
        filled = 0
        for at, piece in enumerate(pieces):
            halved = piece.shape[1] < KVH * 2 * HD
            start = pl.multiple_of((kv_head // 2 if halved else kv_head) * (2 * HD), 2 * HD)
            copies.append(
                pltpu.make_async_copy(
                    piece.at[:, pl.ds(start, 2 * HD)],
                    tokens.at[group, filled : filled + piece.shape[0], :],
                    semaphores.at[group, at],
                )
            )
            filled += piece.shape[0]
    load_copies = weight_copies(weight, weight_out, weight_semaphores, weight_masks)
    if masks[0] == 0:
        query_copy = pltpu.make_async_copy(queries[0], own_queries, query_semaphore)
        query_copy.start()
    for copy in copies + load_copies:
        copy.start()
    if masks[0] == 0:
        query_copy.wait()

    use = use_ref[...][None]
    lane = lax.broadcasted_iota(jnp.int32, (rows, HD), 1)
    factor = LOG2E / math.sqrt(HD)
    for group in range(groups):
        for copy in copies[group * piece_count : (group + 1) * piece_count]:
            copy.wait()
        blocks = []
        for at in range(group * per, group * per + per):
            block = own_queries if masks[at] == 0 else queries[at]
            blocks += [block[:, head * HD : (head + 1) * HD] for head in range(heads_per)]
        stacked = jnp.concatenate(blocks, axis=0)
        scores = lax.dot_general(
            stacked,
            tokens[group, :, :HD],
            (((1,), (1,)), ((), ())),
            preferred_element_type=jnp.float32,
        )
        scores = scores.reshape(GROUP, rows, columns)
        scores = jnp.where(use > 0.0, scores, MASKED)
        row_max = jnp.max(scores, axis=-1, keepdims=True)
        expo = jnp.exp2((scores - row_max) * factor) * use
        total = jnp.sum(expo, axis=-1, keepdims=True)
        weighted = jnp.dot(
            expo.astype(jnp.bfloat16).reshape(GROUP * rows, columns),
            tokens[group, :, HD:],
            preferred_element_type=jnp.float32,
        )
        weighted = (weighted.reshape(GROUP, rows, HD) / total).astype(jnp.bfloat16)
        level = row_max * factor + jnp.log2(total)
        for low in range(per):
            out = parts[group * per + low]
            levels = jnp.zeros((rows, HD), jnp.float32)
            for head in range(heads_per):
                at = low * heads_per + head
                out[:, head * HD : (head + 1) * HD] = weighted[at]
                levels = jnp.where(lane % heads_per == head, level[at], levels)
            out[:, heads_per * HD :] = packed_level(levels, lane, heads_per)
    for copy in load_copies:
        copy.wait()


def combined(parts, heads_per):
    levels = []
    for part in parts:
        level = part[:, heads_per * HD :].astype(jnp.float32)
        levels.append(
            level
            + pltpu.roll(level, HD - heads_per, 1)
            + pltpu.roll(level, HD - 2 * heads_per, 1)
        )
    top = functools.reduce(jnp.maximum, levels)
    shares = [jnp.exp2(level - top) for level in levels]
    total = sum(shares[1:], shares[0])
    shares = [share / total for share in shares]
    heads = []
    for head in range(heads_per):
        terms = [
            share[:, head : head + 1] * part[:, head * HD : (head + 1) * HD].astype(jnp.float32)
            for share, part in zip(shares, parts)
        ]
        heads.append(sum(terms[1:], terms[0]).astype(jnp.bfloat16))
    return jnp.concatenate(heads, axis=1)


def project(rows, weights, out):
    at = 0
    for weight in weights:
        for block in range(weight.shape[0]):
            product = jnp.dot(rows, weight[block], preferred_element_type=jnp.float32)
            out[at] = product.astype(out.dtype)
            at += 1


def project_away_kernel(heads_per, part_count, *refs):
    parts, (*weights, out, attended) = refs[:part_count], refs[part_count:]
    rows = combined(parts, heads_per)
    attended[...] = rows
    project(rows, weights, out)


def project_home_kernel(attended, *refs):
    project(attended[...], refs[:-1], refs[-1])


def add_kernel(home, sibling, *outputs):
    for at, out in enumerate(outputs):
        out[...] = (home[at + 1] + sibling[at + 1].astype(jnp.float32)).astype(out.dtype)


def local(hidden_in, queries, new_kv, kv_pages, out_weight, move_pages, page_table, lengths):
    tensor_count = lax.axis_size("tensor")
    inst_count = lax.axis_size("inst")
    section_rank = lax.axis_index("section")
    per = max(1, tensor_count // KVH)
    heads_per = HEADS // tensor_count
    requests, slots = page_table.shape
    rows = requests * STEPS
    own_pages = kv_pages[0]
    pages, page_tokens, width = own_pages.shape
    capacity = move_pages.shape[2]
    moves = in_hbm(move_pages.reshape(-1))
    depth, features = out_weight.shape[1:]
    chunk = features // tensor_count
    half = tensor_count // 2
    vmem = pl.BlockSpec(memory_space=pltpu.VMEM)
    hbm = pl.BlockSpec(memory_space=pltpu.HBM)
    anywhere = pl.BlockSpec(memory_space=pl.ANY)
    peers = [mask for mask in range(tensor_count) if mask & per == 0]

    if len(peers) == 4:
        peers = [0, 4, 2, 6]
    home_masks = [2 * mask for mask in range(half)]
    if half == 4:
        home_masks = [0, 4, 2, 6]
    away_masks = [mask ^ 1 for mask in home_masks]
    early = half // 4
    weight = in_hbm(out_weight)

    def weight_shape(count):
        return pltpu.VMEM((count, depth, chunk), jnp.bfloat16)

    own_queries = queries[0]
    all_queries = {mask: swapped(own_queries, mask) for mask in peers[1:]}
    all_queries[0] = in_hbm(own_queries)
    own_flat = own_pages.reshape(pages * page_tokens, width)
    partner_flat = swapped(own_flat, per)
    leaving = pl.pallas_call(
        functools.partial(pick_kernel, capacity),
        out_shape=[jax.ShapeDtypeStruct((capacity, page_tokens, width // 2), jnp.bfloat16)]
        * (2 * (inst_count - 1)),
        in_specs=[hbm] * 2,
        out_specs=[vmem] * (2 * (inst_count - 1)),
        scratch_shapes=[
            pltpu.SMEM(moves.shape, jnp.int32),
            pltpu.SemaphoreType.DMA,
            pltpu.SemaphoreType.DMA(((inst_count - 1) * capacity * KVH,)),
        ],
        compiler_params=pltpu.CompilerParams(vmem_limit_bytes=2 * MEGA),
        name="pick",
    )(moves, in_hbm(own_pages))
    arrived = []
    for shift in range(1, inst_count):
        for other in range(2):
            pairs = [
                (
                    inst * tensor_count + rank,
                    (inst + shift) % inst_count * tensor_count + (rank ^ (per * other)),
                )
                for inst in range(inst_count)
                for rank in range(tensor_count)
            ]
            sent = leaving[2 * (shift - 1) + other].reshape(capacity * page_tokens, width // 2)
            arrived.append(lax.ppermute(sent, ("inst", "tensor"), pairs))
    if page_tokens * capacity % 16:
        arrived = [jnp.concatenate(arrived, axis=0)]
    pieces = [in_hbm(own_flat), partner_flat, *arrived, in_hbm(new_kv[0])]
    piece_specs = [hbm, anywhere, *[anywhere] * len(arrived), hbm]
    columns = sum(piece.shape[0] for piece in pieces)

    use, away_weight = pl.pallas_call(
        functools.partial(count_kernel, (pages, page_tokens, capacity), away_masks),
        out_shape=[jax.ShapeDtypeStruct((rows, columns), jnp.float32), weight_shape(half)],
        in_specs=[hbm] * 4,
        out_specs=[vmem] * 2,
        scratch_shapes=[
            pltpu.SMEM((slots, requests), jnp.int32),
            pltpu.SMEM((requests,), jnp.int32),
            pltpu.SMEM(moves.shape, jnp.int32),
            pltpu.SemaphoreType.DMA((3,)),
            pltpu.SemaphoreType.DMA((half,)),
        ],
        compiler_params=pltpu.CompilerParams(vmem_limit_bytes=2 * MEGA),
        name="count_uses",
    )(in_hbm(page_table.T), in_hbm(lengths), moves, weight)

    part_shape = jax.ShapeDtypeStruct((rows, heads_per * HD + HD), jnp.bfloat16)

    def attend(masks, weight_masks):
        groups = len(masks) // per
        *parts, moved_weight = pl.pallas_call(
            functools.partial(attend_kernel, masks, weight_masks, len(pieces)),
            out_shape=[part_shape] * len(masks)
            + [weight_shape(len(weight_masks))],
            in_specs=[vmem] + [vmem if mask else hbm for mask in masks] + piece_specs + [hbm],
            out_specs=[vmem] * (len(masks) + 1),
            scratch_shapes=[
                pltpu.VMEM((rows, heads_per * HD), jnp.bfloat16),
                pltpu.VMEM((groups, columns, 2 * HD), jnp.bfloat16),
                pltpu.SemaphoreType.DMA,
                pltpu.SemaphoreType.DMA((groups, len(pieces))),
                pltpu.SemaphoreType.DMA((len(weight_masks),)),
            ],
            compiler_params=pltpu.CompilerParams(vmem_limit_bytes=8 * MEGA),
            name="attend",
        )(use, *[all_queries[mask] for mask in masks], *pieces, weight)
        return dict(zip(masks, parts)), moved_weight

    parts, home_first = attend(peers[per:], home_masks[:early])
    received = {mask: swapped(part, mask) for mask, part in parts.items()}
    parts, home_second = attend(peers[:per], home_masks[early:])
    received.update({mask: swapped(part, mask) for mask, part in parts.items() if mask})
    received = [parts[0]] + [received[mask] for mask in peers[1:]]

    project_params = pltpu.CompilerParams(vmem_limit_bytes=4 * MEGA)
    away, attended = pl.pallas_call(
        functools.partial(project_away_kernel, heads_per, half),
        in_specs=[vmem] * (half + 1),
        out_specs=[vmem] * 2,
        out_shape=[
            jax.ShapeDtypeStruct((half, rows, chunk), jnp.bfloat16),
            jax.ShapeDtypeStruct((rows, depth), jnp.bfloat16),
        ],
        compiler_params=project_params,
        name="project_away",
    )(*received, away_weight)
    sibling = swapped(away, 1)
    home = pl.pallas_call(
        project_home_kernel,
        in_specs=[vmem] * 3,
        out_specs=vmem,
        out_shape=jax.ShapeDtypeStruct((half, rows, chunk), jnp.float32),
        compiler_params=project_params,
        name="project_home",
    )(attended, home_first, home_second)
    sums = pl.pallas_call(
        add_kernel,
        in_specs=[vmem] * 2,
        out_specs=[vmem] * (half - 1),
        out_shape=[jax.ShapeDtypeStruct((rows, chunk), jnp.bfloat16)] * (half - 1),
        compiler_params=pltpu.CompilerParams(vmem_limit_bytes=2 * MEGA),
        name="add_sibling",
    )(home, sibling)
    projected = home[0] + sibling[0].astype(jnp.float32)
    for mask, total in zip(home_masks[1:], sums):
        projected = projected + swapped(total, mask).astype(jnp.float32)
    after_first = (hidden_in.astype(jnp.float32) + projected).astype(jnp.bfloat16)
    handed_over = lax.ppermute(after_first, "section", [(0, 1), (1, 0)])
    after_second = (handed_over.astype(jnp.float32) + projected).astype(jnp.bfloat16)
    result = jnp.where(section_rank == 0, after_first, after_second)
    return result[None]


def solution(mesh):
    return jax.shard_map(
        local,
        mesh=mesh,
        in_specs=(
            P("inst", "tensor"),
            P("section", "inst", "tensor"),
            P("section", "inst", None),
            P("section", "inst", "tensor", None),
            P("section", "tensor", None),
            P("inst", None, None),
            P("inst", None),
            P("inst"),
        ),
        out_specs=P("section", "inst", "tensor"),
        check_vma=False,
    )
```

```python
import functools
import math

import jax
import jax.numpy as jnp
from jax import lax
from jax.experimental import pallas as pl
from jax.experimental.pallas import tpu as pltpu
from jax.sharding import PartitionSpec as P

HEADS = 64
KVH = 8
HD = 128
STEPS = 4
GROUP = HEADS // KVH
MASKED = -1e30
LOG2E = 1.4426950408889634
FACTOR = LOG2E / math.sqrt(HD)
MEGA = 1024 * 1024
LOAD_SHARES = (1, 3, 0, 0, 3, 1)


def swapped(value, mask):
    count = lax.axis_size("tensor")
    return lax.ppermute(value, "tensor", [(source, source ^ mask) for source in range(count)])


def in_hbm(value):
    return pltpu.with_memory_space_constraint(value, pltpu.HBM)


def place_kernel(place):
    place[0] = lax.axis_index("tensor")
    place[1] = lax.axis_index("inst")


def beside_copies(place):
    return pl.when(place[0] >= 0)


def weight_copies(place, weight, out, semaphores, masks):
    rank = place[0]
    chunk = out.shape[2]
    copies = []
    for at, mask in enumerate(masks):
        start = pl.multiple_of((rank ^ mask) * chunk, chunk)
        copies.append(
            pltpu.make_async_copy(
                weight.at[0, :, pl.ds(start, chunk)], out.at[at], semaphores.at[at]
            )
        )
    return copies


def pick_kernel(capacity, weight_masks, place, moves_hbm, pages, weight, *refs):
    outputs, refs = refs[:-5], refs[-5:]
    weight_out, moves, moves_semaphore, semaphores, weight_semaphores = refs
    moves_copy = pltpu.make_async_copy(moves_hbm, moves, moves_semaphore)
    load_copies = weight_copies(place, weight, weight_out, weight_semaphores, weight_masks)
    for copy in [moves_copy] + load_copies:
        copy.start()
    moves_copy.wait()
    tensor_count, inst_count = lax.axis_size("tensor"), lax.axis_size("inst")
    per = max(1, tensor_count // KVH)
    side = place[0] // per % 2
    copies = []
    for shift in range(1, inst_count):
        target = place[1] + shift
        target = jnp.where(target >= inst_count, target - inst_count, target)
        for slot in range(capacity):
            page = moves[target * capacity + slot]
            for other in range(2):
                out = outputs[2 * (shift - 1) + other]
                for pair in range(KVH // 2):
                    head = 2 * pair + (side if other == 0 else 1 - side)
                    start = pl.multiple_of(head * (2 * HD), 2 * HD)
                    copies.append(
                        pltpu.make_async_copy(
                            pages.at[page, :, pl.ds(start, 2 * HD)],
                            out.at[slot, :, 2 * HD * pair : 2 * HD * (pair + 1)],
                            semaphores.at[len(copies)],
                        )
                    )
    for copy in copies:
        copy.start()
    for copy in copies + load_copies:
        copy.wait()


def packed_level(level, lane, heads_per):
    top = level.astype(jnp.bfloat16).astype(jnp.float32)
    rest = level - top
    middle = rest.astype(jnp.bfloat16).astype(jnp.float32)
    level = jnp.where(lane < heads_per, top, jnp.where(lane < 2 * heads_per, middle, rest - middle))
    return level.astype(jnp.bfloat16)


def prepare_kernel(shape, weight_masks, place, table_hbm, lengths_hbm, moves_hbm, weight, *refs):
    owned, refs = refs[:3], refs[4:]
    bias_out, owned_out, refs = refs[0], refs[1:4], refs[4:]
    weight_out, table, lengths, moves, semaphores, weight_semaphores = refs
    pages, page_tokens, capacity = shape
    tensor_count, inst_count = lax.axis_size("tensor"), lax.axis_size("inst")
    tensor_rank, inst_rank = place[0], place[1]
    per = max(1, tensor_count // KVH)
    partner = tensor_rank ^ per
    rows, columns = bias_out.shape
    slots, requests = table.shape
    page_size = page_tokens * tensor_count
    copies = [
        pltpu.make_async_copy(source, target, semaphores.at[at])
        for at, (source, target) in enumerate(
            ((table_hbm, table), (lengths_hbm, lengths), (moves_hbm, moves))
        )
    ]
    load_copies = [
        pltpu.make_async_copy(source, target, semaphores.at[3 + at])
        for at, (source, target) in enumerate(zip(owned, owned_out))
    ] + weight_copies(place, weight, weight_out, weight_semaphores, weight_masks)
    for copy in copies + load_copies:
        copy.start()
    for copy in copies:
        copy.wait()

    @beside_copies(place)
    def _():
        row = lax.broadcasted_iota(jnp.int32, (rows, 1), 0)
        row_request, row_step = row // STEPS, row % STEPS
        row_length = jnp.zeros((rows, 1), jnp.int32)
        row_pages = [jnp.zeros((rows, 1), jnp.int32) for _ in range(slots)]
        for request in range(requests):
            here = row_request == request
            row_length = jnp.where(here, lengths[request], row_length)
            for slot in range(slots):
                page = table[slot, request]
                arrived = page - pages
                for own in range(capacity):
                    page = jnp.where(
                        arrived == inst_rank * capacity + own, moves[inst_rank * capacity + own], page
                    )
                row_pages[slot] = jnp.where(here, page, row_pages[slot])

        column = lax.broadcasted_iota(jnp.int32, (1, columns), 1)
        own_columns = pages * page_tokens
        block_columns = capacity * page_tokens
        moved = column - 2 * own_columns
        block = moved // block_columns
        source = inst_rank - block // 2 - 1
        source = jnp.where(source < 0, source + inst_count, source)
        resident = moved < 0
        page = jnp.where(
            resident,
            column % own_columns // page_tokens,
            pages + source * capacity + moved // page_tokens % capacity,
        )
        side = jnp.where(resident, column // own_columns, block % 2)
        token = jnp.where(side == 0, tensor_rank, partner) * page_tokens + column % page_tokens
        use = jnp.zeros((rows, columns), jnp.float32)
        for slot in range(slots):
            live = (row_pages[slot] == page) & (token + slot * page_size < row_length)
            use = use + jnp.where(live, 1.0, 0.0)
        fresh = column - (columns - rows)
        fresh_live = (fresh // STEPS == row_request) & (fresh % STEPS <= row_step)
        fresh_live = fresh_live & ((tensor_rank == 0) | (tensor_rank == per))
        use = jnp.where(fresh >= 0, jnp.where(fresh_live, 1.0, 0.0), use)
        bias_out[...] = jnp.where(use > 0.0, jnp.log2(jnp.maximum(use, 1.0)) / FACTOR, MASKED)

    for copy in load_copies:
        copy.wait()


def attend_kernel(masks, weight_masks, piece_count, after_count, *refs):
    place, bias_ref, refs = refs[0], refs[1], refs[2:]
    tensor_count, tensor_rank = lax.axis_size("tensor"), place[0]
    queries, refs = refs[: len(masks)], refs[len(masks) :]
    pieces, refs = refs[:piece_count], refs[piece_count + after_count :]
    if weight_masks:
        weight, *refs, weight_out, weight_semaphores = refs
    parts = refs
    per = max(1, tensor_count // KVH)
    rows = bias_ref.shape[0]
    heads_per = HEADS // tensor_count
    groups = len(masks) // per

    load_copies = []
    if weight_masks:
        load_copies = weight_copies(place, weight, weight_out, weight_semaphores, weight_masks)
    for copy in load_copies:
        copy.start()

    @beside_copies(place)
    def _():
        bias = bias_ref[...]
        lane = lax.broadcasted_iota(jnp.int32, (rows, HD), 1)
        for group in range(groups):
            kv_head = (tensor_rank ^ masks[group * per]) // per
            keys, values = [], []
            for piece in pieces:
                halved = piece.shape[1] < KVH * 2 * HD
                start = pl.multiple_of((kv_head // 2 if halved else kv_head) * (2 * HD), 2 * HD)
                keys.append(piece[:, pl.ds(start, HD)])
                values.append(piece[:, pl.ds(pl.multiple_of(start + HD, HD), HD)])
            blocks = []
            for block in queries[group * per : group * per + per]:
                blocks += [block[:, head * HD : (head + 1) * HD] for head in range(heads_per)]
            stacked = jnp.concatenate(blocks, axis=0)
            scores = lax.dot_general(
                stacked,
                jnp.concatenate(keys, axis=0),
                (((1,), (1,)), ((), ())),
                preferred_element_type=jnp.float32,
            )
            weights, totals, level = [], [], []
            for at in range(GROUP):
                shifted = scores[at * rows : (at + 1) * rows] + bias
                row_max = jnp.max(shifted, axis=1, keepdims=True)
                expo = jnp.exp2((shifted - row_max) * FACTOR)
                total = jnp.sum(expo, axis=1, keepdims=True)
                weights.append(expo.astype(jnp.bfloat16))
                totals.append(total)
                level.append(row_max * FACTOR + jnp.log2(total))
            weighted = jnp.dot(
                jnp.concatenate(weights, axis=0),
                jnp.concatenate(values, axis=0),
                preferred_element_type=jnp.float32,
            )
            for low in range(per):
                out = parts[group * per + low]
                levels = jnp.zeros((rows, HD), jnp.float32)
                for head in range(heads_per):
                    at = low * heads_per + head
                    attended = weighted[at * rows : (at + 1) * rows] / totals[at]
                    out[:, head * HD : (head + 1) * HD] = attended.astype(jnp.bfloat16)
                    levels = jnp.where(lane % heads_per == head, level[at], levels)
                out[:, heads_per * HD :] = packed_level(levels, lane, heads_per)

    for copy in load_copies:
        copy.wait()


def combined(parts, heads_per):
    levels = []
    for part in parts:
        level = part[:, heads_per * HD :].astype(jnp.float32)
        levels.append(
            level
            + pltpu.roll(level, HD - heads_per, 1)
            + pltpu.roll(level, HD - 2 * heads_per, 1)
        )
    top = functools.reduce(jnp.maximum, levels)
    shares = [jnp.exp2(level - top) for level in levels]
    total = sum(shares[1:], shares[0])
    shares = [share / total for share in shares]
    heads = []
    for head in range(heads_per):
        terms = [
            share[:, head : head + 1] * part[:, head * HD : (head + 1) * HD].astype(jnp.float32)
            for share, part in zip(shares, parts)
        ]
        heads.append(sum(terms[1:], terms[0]).astype(jnp.bfloat16))
    return jnp.concatenate(heads, axis=1)


def project(rows, weights, found, out):
    for at, (array, block) in enumerate(found):
        product = jnp.dot(rows, weights[array][block], preferred_element_type=jnp.float32)
        out[at] = product.astype(out.dtype)


def project_away_kernel(heads_per, part_count, found, weight_masks, place, *refs):
    parts, refs = refs[:part_count], refs[part_count:]
    load_copies = []
    if weight_masks:
        *refs, weight_out, weight_semaphores = refs
        weight, refs = refs[0], refs[1:]
        load_copies = weight_copies(place, weight, weight_out, weight_semaphores, weight_masks)
    *weights, out, attended = refs
    for copy in load_copies:
        copy.start()

    @beside_copies(place)
    def _():
        rows = combined(parts, heads_per)
        attended[...] = rows
        project(rows, weights, found, out)

    for copy in load_copies:
        copy.wait()


def project_home_kernel(found, attended, *refs):
    project(attended[...], refs[:-1], found, refs[-1])


def add_far_kernel(home, sibling, out):
    out[...] = (home[1] + sibling[1].astype(jnp.float32)).astype(out.dtype)


def add_own_kernel(home, sibling, far, out):
    own = home[0] + sibling[0].astype(jnp.float32)
    out[...] = own + far[...].astype(jnp.float32)


def project_near_kernel(found, attended, sibling, after, *refs):
    weights, outputs = refs[: len(refs) - len(found)], refs[len(refs) - len(found) :]
    rows = attended[...]
    for at, (array, block) in enumerate(found):
        product = jnp.dot(rows, weights[array][block], preferred_element_type=jnp.float32)
        total = product + sibling[at + 2].astype(jnp.float32)
        outputs[at][...] = total.astype(outputs[at].dtype)


def local(hidden_in, queries, new_kv, kv_pages, out_weight, move_pages, page_table, lengths):
    tensor_count = lax.axis_size("tensor")
    inst_count = lax.axis_size("inst")
    section_rank = lax.axis_index("section")
    per = max(1, tensor_count // KVH)
    heads_per = HEADS // tensor_count
    requests, slots = page_table.shape
    rows = requests * STEPS
    own_pages = kv_pages[0]
    pages, page_tokens, width = own_pages.shape
    capacity = move_pages.shape[2]
    moves = in_hbm(move_pages.reshape(-1))
    depth, features = out_weight.shape[1:]
    chunk = features // tensor_count
    half = tensor_count // 2
    vmem = pl.BlockSpec(memory_space=pltpu.VMEM)
    hbm = pl.BlockSpec(memory_space=pltpu.HBM)
    peers = [mask for mask in range(tensor_count) if mask & per == 0]

    if len(peers) == 4:
        peers = [0, 6, 4, 2]
    home_masks = [2 * mask for mask in range(half)]
    if half == 4:
        home_masks = [0, 6, 4, 2]
    away_masks = [mask ^ 1 for mask in home_masks]
    unit = tensor_count // 8
    loads, filled = [], 0
    for share in LOAD_SHARES:
        loads.append((away_masks + home_masks)[filled : filled + share * unit])
        filled += share * unit
    moved_weights = []

    def weight_parts(wanted):
        arrays = [
            (masks, array) for masks, array in zip(loads, moved_weights) if set(masks) & set(wanted)
        ]
        found = [
            (at, masks.index(mask))
            for mask in wanted
            for at, (masks, _) in enumerate(arrays)
            if mask in masks
        ]
        return [array for _, array in arrays], found

    weight = in_hbm(out_weight)

    def weight_shape(count):
        return pltpu.VMEM((count, depth, chunk), jnp.bfloat16)

    smem = pl.BlockSpec(memory_space=pltpu.SMEM)
    place = pl.pallas_call(
        place_kernel,
        out_shape=pltpu.SMEM((2,), jnp.int32),
        out_specs=smem,
        name="place",
    )()

    own_queries = queries[0]
    all_queries = {mask: swapped(own_queries, mask) for mask in peers[1:]}
    own_flat = own_pages.reshape(pages * page_tokens, width)
    partner_flat = swapped(own_flat, per)
    *leaving, moved = pl.pallas_call(
        functools.partial(pick_kernel, capacity, loads[0]),
        out_shape=[jax.ShapeDtypeStruct((capacity, page_tokens, width // 2), jnp.bfloat16)]
        * (2 * (inst_count - 1))
        + [weight_shape(len(loads[0]))],
        in_specs=[smem] + [hbm] * 3,
        out_specs=[vmem] * (2 * inst_count - 1),
        scratch_shapes=[
            pltpu.SMEM(moves.shape, jnp.int32),
            pltpu.SemaphoreType.DMA,
            pltpu.SemaphoreType.DMA(((inst_count - 1) * capacity * KVH,)),
            pltpu.SemaphoreType.DMA((len(loads[0]),)),
        ],
        compiler_params=pltpu.CompilerParams(vmem_limit_bytes=2 * MEGA),
        name="pick",
    )(place, moves, in_hbm(own_pages), weight)
    moved_weights.append(moved)
    arrived = []
    for shift in range(1, inst_count):
        for other in range(2):
            pairs = [
                (
                    inst * tensor_count + rank,
                    (inst + shift) % inst_count * tensor_count + (rank ^ (per * other)),
                )
                for inst in range(inst_count)
                for rank in range(tensor_count)
            ]
            sent = leaving[2 * (shift - 1) + other].reshape(capacity * page_tokens, width // 2)
            arrived.append(lax.ppermute(sent, ("inst", "tensor"), pairs))
    if page_tokens * capacity % 16:
        arrived = [jnp.concatenate(arrived, axis=0)]
    owned = [own_queries, own_flat, new_kv[0]]
    columns = 2 * own_flat.shape[0] + sum(piece.shape[0] for piece in arrived) + rows

    bias, all_queries[0], own_tokens, new_tokens, moved = pl.pallas_call(
        functools.partial(
            prepare_kernel, (pages, page_tokens, capacity), loads[1]
        ),
        out_shape=[jax.ShapeDtypeStruct((rows, columns), jnp.float32)]
        + [pltpu.VMEM(value.shape, value.dtype) for value in owned]
        + [weight_shape(len(loads[1]))],
        in_specs=[smem] + [hbm] * 7 + [vmem],
        out_specs=[vmem] * 5,
        scratch_shapes=[
            pltpu.SMEM((slots, requests), jnp.int32),
            pltpu.SMEM((requests,), jnp.int32),
            pltpu.SMEM(moves.shape, jnp.int32),
            pltpu.SemaphoreType.DMA((6,)),
            pltpu.SemaphoreType.DMA((len(loads[1]),)),
        ],
        compiler_params=pltpu.CompilerParams(vmem_limit_bytes=2 * MEGA),
        name="prepare",
    )(
        place,
        in_hbm(page_table.T),
        in_hbm(lengths),
        moves,
        weight,
        *[in_hbm(value) for value in owned],
        all_queries[peers[per]],
    )
    moved_weights.append(moved)
    pieces = [own_tokens, partner_flat, *arrived, new_tokens]

    part_shape = jax.ShapeDtypeStruct((rows, heads_per * HD + HD), jnp.bfloat16)

    def attend(masks, weight_masks, *after):
        loading = bool(weight_masks)
        results = pl.pallas_call(
            functools.partial(attend_kernel, masks, weight_masks, len(pieces), len(after)),
            out_shape=[part_shape] * len(masks) + [weight_shape(len(weight_masks))] * loading,
            in_specs=[smem] + [vmem] * (1 + len(masks) + len(pieces) + len(after)) + [hbm] * loading,
            out_specs=[vmem] * (len(masks) + loading),
            scratch_shapes=[pltpu.SemaphoreType.DMA((len(weight_masks),))] * loading,
            compiler_params=pltpu.CompilerParams(vmem_limit_bytes=8 * MEGA),
            name="attend",
        )(place, bias, *[all_queries[mask] for mask in masks], *pieces, *after, *[weight] * loading)
        moved_weights.append(results[-1] if loading else None)
        return dict(zip(masks, results))

    received, after = {}, []
    for masks, weight_masks in (
        (peers[per : 2 * per], loads[2]),
        (peers[2 * per :], loads[3]),
        (peers[:per], loads[4]),
    ):
        parts = attend(masks, weight_masks, *after)
        after = [received[peers[per]] if received else parts[masks[0]]]
        received.update({mask: swapped(part, mask) for mask, part in parts.items() if mask})
    received = [parts[0]] + [received[mask] for mask in peers[1:]]

    project_params = pltpu.CompilerParams(vmem_limit_bytes=4 * MEGA)
    loading = bool(loads[5])
    away_weights, found = weight_parts(away_masks)
    away, attended, *moved = pl.pallas_call(
        functools.partial(project_away_kernel, heads_per, half, found, loads[5]),
        in_specs=[smem] + [vmem] * half + [hbm] * loading + [vmem] * len(away_weights),
        out_specs=[vmem] * (2 + loading),
        out_shape=[
            jax.ShapeDtypeStruct((half, rows, chunk), jnp.bfloat16),
            jax.ShapeDtypeStruct((rows, depth), jnp.bfloat16),
        ]
        + [weight_shape(len(loads[5]))] * loading,
        scratch_shapes=[pltpu.SemaphoreType.DMA((len(loads[5]),))] * loading,
        compiler_params=project_params,
        name="project_away",
    )(place, *received, *[weight] * loading, *away_weights)
    moved_weights.extend(moved)
    sibling = swapped(away, 1)
    home_weights, found = weight_parts(home_masks[:2])
    home = pl.pallas_call(
        functools.partial(project_home_kernel, found),
        in_specs=[vmem] * (1 + len(home_weights)),
        out_specs=vmem,
        out_shape=jax.ShapeDtypeStruct((2, rows, chunk), jnp.float32),
        compiler_params=project_params,
        name="project_home",
    )(attended, *home_weights)
    sum_shape = jax.ShapeDtypeStruct((rows, chunk), jnp.bfloat16)
    far_sum = pl.pallas_call(
        add_far_kernel,
        in_specs=[vmem] * 2,
        out_specs=vmem,
        out_shape=sum_shape,
        compiler_params=pltpu.CompilerParams(vmem_limit_bytes=2 * MEGA),
        name="add_far",
    )(home, sibling)
    home_weights, found = weight_parts(home_masks[2:])
    near_sums = pl.pallas_call(
        functools.partial(project_near_kernel, found),
        in_specs=[vmem] * (3 + len(home_weights)),
        out_specs=[vmem] * (half - 2),
        out_shape=[sum_shape] * (half - 2),
        compiler_params=project_params,
        name="project_near",
    )(attended, sibling, far_sum, *home_weights)
    projected = pl.pallas_call(
        add_own_kernel,
        in_specs=[vmem] * 3,
        out_specs=vmem,
        out_shape=jax.ShapeDtypeStruct((rows, chunk), jnp.float32),
        compiler_params=pltpu.CompilerParams(vmem_limit_bytes=2 * MEGA),
        name="add_own",
    )(home, sibling, swapped(far_sum, home_masks[1]))
    for mask, total in zip(home_masks[2:], near_sums):
        projected = projected + swapped(total, mask).astype(jnp.float32)
    after_first = (hidden_in.astype(jnp.float32) + projected).astype(jnp.bfloat16)
    handed_over = lax.ppermute(after_first, "section", [(0, 1), (1, 0)])
    after_second = (handed_over.astype(jnp.float32) + projected).astype(jnp.bfloat16)
    result = jnp.where(section_rank == 0, after_first, after_second)
    return result[None]


def solution(mesh):
    return jax.shard_map(
        local,
        mesh=mesh,
        in_specs=(
            P("inst", "tensor"),
            P("section", "inst", "tensor"),
            P("section", "inst", None),
            P("section", "inst", "tensor", None),
            P("section", "tensor", None),
            P("inst", None, None),
            P("inst", None),
            P("inst"),
        ),
        out_specs=P("section", "inst", "tensor"),
        check_vma=False,
    )
```

```python
import functools
import math

import jax
import jax.numpy as jnp
from jax import lax
from jax.experimental import pallas as pl
from jax.experimental.pallas import tpu as pltpu
from jax.sharding import PartitionSpec as P

HEADS = 64
KVH = 8
HD = 128
STEPS = 4
GROUP = HEADS // KVH
MASKED = -1e30
LOG2E = 1.4426950408889634
FACTOR = LOG2E / math.sqrt(HD)
MEGA = 1024 * 1024
LOAD_SHARES = (1, 1, 0, 1, 4, 1)


def swapped(value, mask):
    count = lax.axis_size("tensor")
    return lax.ppermute(value, "tensor", [(source, source ^ mask) for source in range(count)])


def in_hbm(value):
    return pltpu.with_memory_space_constraint(value, pltpu.HBM)


def place_kernel(place):
    place[0] = lax.axis_index("tensor")
    place[1] = lax.axis_index("inst")


def beside_copies(place):
    return pl.when(place[0] >= 0)


def weight_copies(place, weight, out, semaphores, masks):
    rank = place[0]
    chunk = out.shape[2]
    copies = []
    for at, mask in enumerate(masks):
        start = pl.multiple_of((rank ^ mask) * chunk, chunk)
        copies.append(
            pltpu.make_async_copy(
                weight.at[0, :, pl.ds(start, chunk)], out.at[at], semaphores.at[at]
            )
        )
    return copies


def pick_kernel(capacity, weight_masks, place, moves_hbm, pages, weight, *refs):
    outputs, refs = refs[:-5], refs[-5:]
    weight_out, moves, moves_semaphore, semaphores, weight_semaphores = refs
    moves_copy = pltpu.make_async_copy(moves_hbm, moves, moves_semaphore)
    load_copies = weight_copies(place, weight, weight_out, weight_semaphores, weight_masks)
    for copy in [moves_copy] + load_copies:
        copy.start()
    moves_copy.wait()
    tensor_count, inst_count = lax.axis_size("tensor"), lax.axis_size("inst")
    per = max(1, tensor_count // KVH)
    side = place[0] // per % 2
    copies = []
    for shift in range(1, inst_count):
        target = place[1] + shift
        target = jnp.where(target >= inst_count, target - inst_count, target)
        for slot in range(capacity):
            page = moves[target * capacity + slot]
            for other in range(2):
                out = outputs[2 * (shift - 1) + other]
                for pair in range(KVH // 2):
                    head = 2 * pair + (side if other == 0 else 1 - side)
                    start = pl.multiple_of(head * (2 * HD), 2 * HD)
                    copies.append(
                        pltpu.make_async_copy(
                            pages.at[page, :, pl.ds(start, 2 * HD)],
                            out.at[slot, :, 2 * HD * pair : 2 * HD * (pair + 1)],
                            semaphores.at[len(copies)],
                        )
                    )
    for copy in copies:
        copy.start()
    for copy in copies + load_copies:
        copy.wait()


def packed_level(level, lane, heads_per):
    top = level.astype(jnp.bfloat16).astype(jnp.float32)
    rest = level - top
    middle = rest.astype(jnp.bfloat16).astype(jnp.float32)
    level = jnp.where(lane < heads_per, top, jnp.where(lane < 2 * heads_per, middle, rest - middle))
    return level.astype(jnp.bfloat16)


def prepare_kernel(shape, weight_masks, place, table_hbm, lengths_hbm, moves_hbm, weight, *refs):
    owned, refs = refs[:3], refs[4:]
    bias_out, owned_out, refs = refs[0], refs[1:4], refs[4:]
    weight_out, table, lengths, moves, semaphores, weight_semaphores = refs
    pages, page_tokens, capacity = shape
    tensor_count, inst_count = lax.axis_size("tensor"), lax.axis_size("inst")
    tensor_rank, inst_rank = place[0], place[1]
    per = max(1, tensor_count // KVH)
    partner = tensor_rank ^ per
    rows, columns = bias_out.shape
    slots, requests = table.shape
    page_size = page_tokens * tensor_count
    copies = [
        pltpu.make_async_copy(source, target, semaphores.at[at])
        for at, (source, target) in enumerate(
            ((table_hbm, table), (lengths_hbm, lengths), (moves_hbm, moves))
        )
    ]
    load_copies = [
        pltpu.make_async_copy(source, target, semaphores.at[3 + at])
        for at, (source, target) in enumerate(zip(owned, owned_out))
    ] + weight_copies(place, weight, weight_out, weight_semaphores, weight_masks)
    for copy in copies + load_copies:
        copy.start()
    for copy in copies:
        copy.wait()

    @beside_copies(place)
    def _():
        row = lax.broadcasted_iota(jnp.int32, (rows, 1), 0)
        row_request, row_step = row // STEPS, row % STEPS
        row_length = jnp.zeros((rows, 1), jnp.int32)
        row_pages = [jnp.zeros((rows, 1), jnp.int32) for _ in range(slots)]
        for request in range(requests):
            here = row_request == request
            row_length = jnp.where(here, lengths[request], row_length)
            for slot in range(slots):
                page = table[slot, request]
                arrived = page - pages
                for own in range(capacity):
                    page = jnp.where(
                        arrived == inst_rank * capacity + own, moves[inst_rank * capacity + own], page
                    )
                row_pages[slot] = jnp.where(here, page, row_pages[slot])

        column = lax.broadcasted_iota(jnp.int32, (1, columns), 1)
        own_columns = pages * page_tokens
        block_columns = capacity * page_tokens
        moved = column - 2 * own_columns
        block = moved // block_columns
        source = inst_rank - block // 2 - 1
        source = jnp.where(source < 0, source + inst_count, source)
        resident = moved < 0
        page = jnp.where(
            resident,
            column % own_columns // page_tokens,
            pages + source * capacity + moved // page_tokens % capacity,
        )
        side = jnp.where(resident, column // own_columns, block % 2)
        token = jnp.where(side == 0, tensor_rank, partner) * page_tokens + column % page_tokens
        use = jnp.zeros((rows, columns), jnp.float32)
        for slot in range(slots):
            live = (row_pages[slot] == page) & (token + slot * page_size < row_length)
            use = use + jnp.where(live, 1.0, 0.0)
        fresh = column - (columns - rows)
        fresh_live = (fresh // STEPS == row_request) & (fresh % STEPS <= row_step)
        fresh_live = fresh_live & ((tensor_rank == 0) | (tensor_rank == per))
        use = jnp.where(fresh >= 0, jnp.where(fresh_live, 1.0, 0.0), use)
        bias_out[...] = jnp.where(use > 0.0, jnp.log2(jnp.maximum(use, 1.0)) / FACTOR, MASKED)

    for copy in load_copies:
        copy.wait()


def attend_kernel(masks, weight_masks, piece_count, after_count, *refs):
    place, bias_ref, refs = refs[0], refs[1], refs[2:]
    tensor_count, tensor_rank = lax.axis_size("tensor"), place[0]
    queries, refs = refs[: len(masks)], refs[len(masks) :]
    pieces, refs = refs[:piece_count], refs[piece_count + after_count :]
    if weight_masks:
        weight, *refs, weight_out, weight_semaphores = refs
    parts = refs
    per = max(1, tensor_count // KVH)
    rows = bias_ref.shape[0]
    heads_per = HEADS // tensor_count
    groups = len(masks) // per

    load_copies = []
    if weight_masks:
        load_copies = weight_copies(place, weight, weight_out, weight_semaphores, weight_masks)
    for copy in load_copies:
        copy.start()

    @beside_copies(place)
    def _():
        bias = bias_ref[...]
        lane = lax.broadcasted_iota(jnp.int32, (rows, HD), 1)
        for group in range(groups):
            kv_head = (tensor_rank ^ masks[group * per]) // per
            keys, values = [], []
            for piece in pieces:
                halved = piece.shape[1] < KVH * 2 * HD
                start = pl.multiple_of((kv_head // 2 if halved else kv_head) * (2 * HD), 2 * HD)
                keys.append(piece[:, pl.ds(start, HD)])
                values.append(piece[:, pl.ds(pl.multiple_of(start + HD, HD), HD)])
            blocks = []
            for block in queries[group * per : group * per + per]:
                blocks += [block[:, head * HD : (head + 1) * HD] for head in range(heads_per)]
            stacked = jnp.concatenate(blocks, axis=0)
            scores = lax.dot_general(
                stacked,
                jnp.concatenate(keys, axis=0),
                (((1,), (1,)), ((), ())),
                preferred_element_type=jnp.float32,
            )
            weights, totals, level = [], [], []
            for at in range(GROUP):
                shifted = scores[at * rows : (at + 1) * rows] + bias
                row_max = jnp.max(shifted, axis=1, keepdims=True)
                expo = jnp.exp2((shifted - row_max) * FACTOR)
                total = jnp.sum(expo, axis=1, keepdims=True)
                weights.append(expo.astype(jnp.bfloat16))
                totals.append(total)
                level.append(row_max * FACTOR + jnp.log2(total))
            weighted = jnp.dot(
                jnp.concatenate(weights, axis=0),
                jnp.concatenate(values, axis=0),
                preferred_element_type=jnp.float32,
            )
            for low in range(per):
                out = parts[group * per + low]
                levels = jnp.zeros((rows, HD), jnp.float32)
                for head in range(heads_per):
                    at = low * heads_per + head
                    attended = weighted[at * rows : (at + 1) * rows] / totals[at]
                    out[:, head * HD : (head + 1) * HD] = attended.astype(jnp.bfloat16)
                    levels = jnp.where(lane % heads_per == head, level[at], levels)
                out[:, heads_per * HD :] = packed_level(levels, lane, heads_per)

    for copy in load_copies:
        copy.wait()


def combined(parts, heads_per):
    levels = []
    for part in parts:
        level = part[:, heads_per * HD :].astype(jnp.float32)
        levels.append(
            level
            + pltpu.roll(level, HD - heads_per, 1)
            + pltpu.roll(level, HD - 2 * heads_per, 1)
        )
    top = functools.reduce(jnp.maximum, levels)
    shares = [jnp.exp2(level - top) for level in levels]
    total = sum(shares[1:], shares[0])
    shares = [share / total for share in shares]
    heads = []
    for head in range(heads_per):
        terms = [
            share[:, head : head + 1] * part[:, head * HD : (head + 1) * HD].astype(jnp.float32)
            for share, part in zip(shares, parts)
        ]
        heads.append(sum(terms[1:], terms[0]).astype(jnp.bfloat16))
    return jnp.concatenate(heads, axis=1)


def project(rows, weights, found, out):
    for at, (array, block) in enumerate(found):
        product = jnp.dot(rows, weights[array][block], preferred_element_type=jnp.float32)
        out[at] = product.astype(out.dtype)


def project_away_kernel(heads_per, part_count, found, weight_masks, place, *refs):
    parts, refs = refs[:part_count], refs[part_count:]
    load_copies = []
    if weight_masks:
        *refs, weight_out, weight_semaphores = refs
        weight, refs = refs[0], refs[1:]
        load_copies = weight_copies(place, weight, weight_out, weight_semaphores, weight_masks)
    *weights, out, attended = refs
    for copy in load_copies:
        copy.start()

    @beside_copies(place)
    def _():
        rows = combined(parts, heads_per)
        attended[...] = rows
        project(rows, weights, found, out)

    for copy in load_copies:
        copy.wait()


def project_home_kernel(found, attended, *refs):
    project(attended[...], refs[:-1], found, refs[-1])


def add_far_kernel(home, sibling, out):
    out[...] = (home[1] + sibling[1].astype(jnp.float32)).astype(out.dtype)


def add_own_kernel(home, sibling, far, out):
    own = home[0] + sibling[0].astype(jnp.float32)
    out[...] = own + far[...].astype(jnp.float32)


def project_near_kernel(found, attended, sibling, after, *refs):
    weights, outputs = refs[: len(refs) - len(found)], refs[len(refs) - len(found) :]
    rows = attended[...]
    for at, (array, block) in enumerate(found):
        product = jnp.dot(rows, weights[array][block], preferred_element_type=jnp.float32)
        total = product + sibling[at + 2].astype(jnp.float32)
        outputs[at][...] = total.astype(outputs[at].dtype)


def local(hidden_in, queries, new_kv, kv_pages, out_weight, move_pages, page_table, lengths):
    tensor_count = lax.axis_size("tensor")
    inst_count = lax.axis_size("inst")
    section_rank = lax.axis_index("section")
    per = max(1, tensor_count // KVH)
    heads_per = HEADS // tensor_count
    requests, slots = page_table.shape
    rows = requests * STEPS
    own_pages = kv_pages[0]
    pages, page_tokens, width = own_pages.shape
    capacity = move_pages.shape[2]
    moves = in_hbm(move_pages.reshape(-1))
    depth, features = out_weight.shape[1:]
    chunk = features // tensor_count
    half = tensor_count // 2
    vmem = pl.BlockSpec(memory_space=pltpu.VMEM)
    hbm = pl.BlockSpec(memory_space=pltpu.HBM)
    peers = [mask for mask in range(tensor_count) if mask & per == 0]

    if len(peers) == 4:
        peers = [0, 6, 4, 2]
    home_masks = [2 * mask for mask in range(half)]
    if half == 4:
        home_masks = [0, 6, 4, 2]
    away_masks = [mask ^ 1 for mask in home_masks]
    unit = tensor_count // 8
    loads, filled = [], 0
    for share in LOAD_SHARES:
        loads.append((away_masks + home_masks)[filled : filled + share * unit])
        filled += share * unit
    moved_weights = []

    def weight_parts(wanted):
        arrays = [
            (masks, array) for masks, array in zip(loads, moved_weights) if set(masks) & set(wanted)
        ]
        found = [
            (at, masks.index(mask))
            for mask in wanted
            for at, (masks, _) in enumerate(arrays)
            if mask in masks
        ]
        return [array for _, array in arrays], found

    weight = in_hbm(out_weight)

    def weight_shape(count):
        return pltpu.VMEM((count, depth, chunk), jnp.bfloat16)

    smem = pl.BlockSpec(memory_space=pltpu.SMEM)
    place = pl.pallas_call(
        place_kernel,
        out_shape=pltpu.SMEM((2,), jnp.int32),
        out_specs=smem,
        name="place",
    )()

    own_queries = queries[0]
    all_queries = {mask: swapped(own_queries, mask) for mask in peers[1:]}
    own_flat = own_pages.reshape(pages * page_tokens, width)
    partner_flat = swapped(own_flat, per)
    *leaving, moved = pl.pallas_call(
        functools.partial(pick_kernel, capacity, loads[0]),
        out_shape=[jax.ShapeDtypeStruct((capacity, page_tokens, width // 2), jnp.bfloat16)]
        * (2 * (inst_count - 1))
        + [weight_shape(len(loads[0]))],
        in_specs=[smem] + [hbm] * 3,
        out_specs=[vmem] * (2 * inst_count - 1),
        scratch_shapes=[
            pltpu.SMEM(moves.shape, jnp.int32),
            pltpu.SemaphoreType.DMA,
            pltpu.SemaphoreType.DMA(((inst_count - 1) * capacity * KVH,)),
            pltpu.SemaphoreType.DMA((len(loads[0]),)),
        ],
        compiler_params=pltpu.CompilerParams(vmem_limit_bytes=2 * MEGA),
        name="pick",
    )(place, moves, in_hbm(own_pages), weight)
    moved_weights.append(moved)
    arrived = []
    for shift in range(1, inst_count):
        for other in range(2):
            pairs = [
                (
                    inst * tensor_count + rank,
                    (inst + shift) % inst_count * tensor_count + (rank ^ (per * other)),
                )
                for inst in range(inst_count)
                for rank in range(tensor_count)
            ]
            sent = leaving[2 * (shift - 1) + other].reshape(capacity * page_tokens, width // 2)
            arrived.append(lax.ppermute(sent, ("inst", "tensor"), pairs))
    if page_tokens * capacity % 16:
        arrived = [jnp.concatenate(arrived, axis=0)]
    owned = [own_queries, own_flat, new_kv[0]]
    columns = 2 * own_flat.shape[0] + sum(piece.shape[0] for piece in arrived) + rows

    bias, all_queries[0], own_tokens, new_tokens, moved = pl.pallas_call(
        functools.partial(
            prepare_kernel, (pages, page_tokens, capacity), loads[1]
        ),
        out_shape=[jax.ShapeDtypeStruct((rows, columns), jnp.float32)]
        + [pltpu.VMEM(value.shape, value.dtype) for value in owned]
        + [weight_shape(len(loads[1]))],
        in_specs=[smem] + [hbm] * 7 + [vmem],
        out_specs=[vmem] * 5,
        scratch_shapes=[
            pltpu.SMEM((slots, requests), jnp.int32),
            pltpu.SMEM((requests,), jnp.int32),
            pltpu.SMEM(moves.shape, jnp.int32),
            pltpu.SemaphoreType.DMA((6,)),
            pltpu.SemaphoreType.DMA((len(loads[1]),)),
        ],
        compiler_params=pltpu.CompilerParams(vmem_limit_bytes=2 * MEGA),
        name="prepare",
    )(
        place,
        in_hbm(page_table.T),
        in_hbm(lengths),
        moves,
        weight,
        *[in_hbm(value) for value in owned],
        all_queries[peers[per]],
    )
    moved_weights.append(moved)
    pieces = [own_tokens, partner_flat, *arrived, new_tokens]

    part_shape = jax.ShapeDtypeStruct((rows, heads_per * HD + HD), jnp.bfloat16)

    def attend(masks, weight_masks, *after):
        loading = bool(weight_masks)
        results = pl.pallas_call(
            functools.partial(attend_kernel, masks, weight_masks, len(pieces), len(after)),
            out_shape=[part_shape] * len(masks) + [weight_shape(len(weight_masks))] * loading,
            in_specs=[smem] + [vmem] * (1 + len(masks) + len(pieces) + len(after)) + [hbm] * loading,
            out_specs=[vmem] * (len(masks) + loading),
            scratch_shapes=[pltpu.SemaphoreType.DMA((len(weight_masks),))] * loading,
            compiler_params=pltpu.CompilerParams(vmem_limit_bytes=8 * MEGA),
            name="attend",
        )(place, bias, *[all_queries[mask] for mask in masks], *pieces, *after, *[weight] * loading)
        moved_weights.append(results[-1] if loading else None)
        return dict(zip(masks, results))

    received, after = {}, []
    for masks, weight_masks in (
        (peers[per : 2 * per], loads[2]),
        (peers[2 * per :], loads[3]),
        (peers[:per], loads[4]),
    ):
        parts = attend(masks, weight_masks, *after)
        after = [received[peers[per]] if received else parts[masks[0]]]
        received.update({mask: swapped(part, mask) for mask, part in parts.items() if mask})
    received = [parts[0]] + [received[mask] for mask in peers[1:]]

    project_params = pltpu.CompilerParams(vmem_limit_bytes=4 * MEGA)
    loading = bool(loads[5])
    away_weights, found = weight_parts(away_masks)
    away, attended, *moved = pl.pallas_call(
        functools.partial(project_away_kernel, heads_per, half, found, loads[5]),
        in_specs=[smem] + [vmem] * half + [hbm] * loading + [vmem] * len(away_weights),
        out_specs=[vmem] * (2 + loading),
        out_shape=[
            jax.ShapeDtypeStruct((half, rows, chunk), jnp.bfloat16),
            jax.ShapeDtypeStruct((rows, depth), jnp.bfloat16),
        ]
        + [weight_shape(len(loads[5]))] * loading,
        scratch_shapes=[pltpu.SemaphoreType.DMA((len(loads[5]),))] * loading,
        compiler_params=project_params,
        name="project_away",
    )(place, *received, *[weight] * loading, *away_weights)
    moved_weights.extend(moved)
    sibling = swapped(away, 1)
    home_weights, found = weight_parts(home_masks[:2])
    home = pl.pallas_call(
        functools.partial(project_home_kernel, found),
        in_specs=[vmem] * (1 + len(home_weights)),
        out_specs=vmem,
        out_shape=jax.ShapeDtypeStruct((2, rows, chunk), jnp.float32),
        compiler_params=project_params,
        name="project_home",
    )(attended, *home_weights)
    sum_shape = jax.ShapeDtypeStruct((rows, chunk), jnp.bfloat16)
    far_sum = pl.pallas_call(
        add_far_kernel,
        in_specs=[vmem] * 2,
        out_specs=vmem,
        out_shape=sum_shape,
        compiler_params=pltpu.CompilerParams(vmem_limit_bytes=2 * MEGA),
        name="add_far",
    )(home, sibling)
    home_weights, found = weight_parts(home_masks[2:])
    near_sums = pl.pallas_call(
        functools.partial(project_near_kernel, found),
        in_specs=[vmem] * (3 + len(home_weights)),
        out_specs=[vmem] * (half - 2),
        out_shape=[sum_shape] * (half - 2),
        compiler_params=project_params,
        name="project_near",
    )(attended, sibling, far_sum, *home_weights)
    projected = pl.pallas_call(
        add_own_kernel,
        in_specs=[vmem] * 3,
        out_specs=vmem,
        out_shape=jax.ShapeDtypeStruct((rows, chunk), jnp.float32),
        compiler_params=pltpu.CompilerParams(vmem_limit_bytes=2 * MEGA),
        name="add_own",
    )(home, sibling, swapped(far_sum, home_masks[1]))
    for mask, total in zip(home_masks[2:], near_sums):
        projected = projected + swapped(total, mask).astype(jnp.float32)
    after_first = (hidden_in.astype(jnp.float32) + projected).astype(jnp.bfloat16)
    handed_over = lax.ppermute(after_first, "section", [(0, 1), (1, 0)])
    after_second = (handed_over.astype(jnp.float32) + projected).astype(jnp.bfloat16)
    result = jnp.where(section_rank == 0, after_first, after_second)
    return result[None]


def solution(mesh):
    return jax.shard_map(
        local,
        mesh=mesh,
        in_specs=(
            P("inst", "tensor"),
            P("section", "inst", "tensor"),
            P("section", "inst", None),
            P("section", "inst", "tensor", None),
            P("section", "tensor", None),
            P("inst", None, None),
            P("inst", None),
            P("inst"),
        ),
        out_specs=P("section", "inst", "tensor"),
        check_vma=False,
    )
```

```python
import functools
import math

import jax
import jax.numpy as jnp
from jax import lax
from jax.experimental import pallas as pl
from jax.experimental.pallas import tpu as pltpu
from jax.sharding import PartitionSpec as P

HEADS = 64
KVH = 8
HD = 128
STEPS = 4
GROUP = HEADS // KVH
MASKED = -1e30
LOG2E = 1.4426950408889634
FACTOR = LOG2E / math.sqrt(HD)
MEGA = 1024 * 1024
LOAD_SHARES = (1, 1, 0, 1, 4, 1)


def swapped(value, mask):
    count = lax.axis_size("tensor")
    return lax.ppermute(value, "tensor", [(source, source ^ mask) for source in range(count)])


def in_hbm(value):
    return pltpu.with_memory_space_constraint(value, pltpu.HBM)


def place_kernel(place):
    place[0] = lax.axis_index("tensor")
    place[1] = lax.axis_index("inst")


def beside_copies(place):
    return pl.when(place[0] >= 0)


def weight_copies(place, weight, out, semaphores, masks):
    rank = place[0]
    chunk = out.shape[2]
    copies = []
    for at, mask in enumerate(masks):
        start = pl.multiple_of((rank ^ mask) * chunk, chunk)
        copies.append(
            pltpu.make_async_copy(
                weight.at[0, :, pl.ds(start, chunk)], out.at[at], semaphores.at[at]
            )
        )
    return copies


def pick_kernel(capacity, weight_masks, place, moves_hbm, pages, weight, *refs):
    outputs, refs = refs[:-5], refs[-5:]
    weight_out, moves, moves_semaphore, semaphores, weight_semaphores = refs
    moves_copy = pltpu.make_async_copy(moves_hbm, moves, moves_semaphore)
    load_copies = weight_copies(place, weight, weight_out, weight_semaphores, weight_masks)
    for copy in [moves_copy] + load_copies:
        copy.start()
    moves_copy.wait()
    tensor_count, inst_count = lax.axis_size("tensor"), lax.axis_size("inst")
    per = max(1, tensor_count // KVH)
    side = place[0] // per % 2
    copies = []
    for shift in range(1, inst_count):
        target = place[1] + shift
        target = jnp.where(target >= inst_count, target - inst_count, target)
        for slot in range(capacity):
            page = moves[target * capacity + slot]
            for other in range(2):
                out = outputs[2 * (shift - 1) + other]
                for pair in range(KVH // 2):
                    head = 2 * pair + (side if other == 0 else 1 - side)
                    start = pl.multiple_of(head * (2 * HD), 2 * HD)
                    copies.append(
                        pltpu.make_async_copy(
                            pages.at[page, :, pl.ds(start, 2 * HD)],
                            out.at[slot, :, 2 * HD * pair : 2 * HD * (pair + 1)],
                            semaphores.at[len(copies)],
                        )
                    )
    for copy in copies:
        copy.start()
    for copy in copies + load_copies:
        copy.wait()


def packed_level(level, lane, heads_per):
    top = level.astype(jnp.bfloat16).astype(jnp.float32)
    rest = level - top
    middle = rest.astype(jnp.bfloat16).astype(jnp.float32)
    level = jnp.where(lane < heads_per, top, jnp.where(lane < 2 * heads_per, middle, rest - middle))
    return level.astype(jnp.bfloat16)


def prepare_kernel(shape, weight_masks, place, table_hbm, lengths_hbm, moves_hbm, weight, *refs):
    owned, refs = refs[:3], refs[4:]
    bias_out, owned_out, refs = refs[0], refs[1:4], refs[4:]
    weight_out, table, lengths, moves, semaphores, weight_semaphores = refs
    pages, page_tokens, capacity = shape
    tensor_count, inst_count = lax.axis_size("tensor"), lax.axis_size("inst")
    tensor_rank, inst_rank = place[0], place[1]
    per = max(1, tensor_count // KVH)
    partner = tensor_rank ^ per
    rows, columns = bias_out.shape
    slots, requests = table.shape
    page_size = page_tokens * tensor_count
    copies = [
        pltpu.make_async_copy(source, target, semaphores.at[at])
        for at, (source, target) in enumerate(
            ((table_hbm, table), (lengths_hbm, lengths), (moves_hbm, moves))
        )
    ]
    load_copies = [
        pltpu.make_async_copy(source, target, semaphores.at[3 + at])
        for at, (source, target) in enumerate(zip(owned, owned_out))
    ] + weight_copies(place, weight, weight_out, weight_semaphores, weight_masks)
    for copy in copies + load_copies:
        copy.start()
    for copy in copies:
        copy.wait()

    @beside_copies(place)
    def _():
        row = lax.broadcasted_iota(jnp.int32, (rows, 1), 0)
        row_request, row_step = row // STEPS, row % STEPS
        row_length = jnp.zeros((rows, 1), jnp.int32)
        row_pages = [jnp.zeros((rows, 1), jnp.int32) for _ in range(slots)]
        for request in range(requests):
            here = row_request == request
            row_length = jnp.where(here, lengths[request], row_length)
            for slot in range(slots):
                page = table[slot, request]
                arrived = page - pages
                for own in range(capacity):
                    page = jnp.where(
                        arrived == inst_rank * capacity + own, moves[inst_rank * capacity + own], page
                    )
                row_pages[slot] = jnp.where(here, page, row_pages[slot])

        column = lax.broadcasted_iota(jnp.int32, (1, columns), 1)
        own_columns = pages * page_tokens
        block_columns = capacity * page_tokens
        moved = column - 2 * own_columns
        block = moved // block_columns
        source = inst_rank - block // 2 - 1
        source = jnp.where(source < 0, source + inst_count, source)
        resident = moved < 0
        page = jnp.where(
            resident,
            column % own_columns // page_tokens,
            pages + source * capacity + moved // page_tokens % capacity,
        )
        side = jnp.where(resident, column // own_columns, block % 2)
        token = jnp.where(side == 0, tensor_rank, partner) * page_tokens + column % page_tokens
        use = jnp.zeros((rows, columns), jnp.float32)
        for slot in range(slots):
            live = (row_pages[slot] == page) & (token + slot * page_size < row_length)
            use = use + jnp.where(live, 1.0, 0.0)
        fresh = column - (columns - rows)
        fresh_live = (fresh // STEPS == row_request) & (fresh % STEPS <= row_step)
        fresh_live = fresh_live & ((tensor_rank == 0) | (tensor_rank == per))
        use = jnp.where(fresh >= 0, jnp.where(fresh_live, 1.0, 0.0), use)
        bias_out[...] = jnp.where(use > 0.0, jnp.log2(jnp.maximum(use, 1.0)) / FACTOR, MASKED)

    for copy in load_copies:
        copy.wait()


def attend_kernel(masks, weight_masks, piece_count, after_count, *refs):
    place, bias_ref, refs = refs[0], refs[1], refs[2:]
    tensor_count, tensor_rank = lax.axis_size("tensor"), place[0]
    queries, refs = refs[: len(masks)], refs[len(masks) :]
    pieces, refs = refs[:piece_count], refs[piece_count + after_count :]
    if weight_masks:
        weight, *refs, weight_out, weight_semaphores = refs
    parts = refs
    per = max(1, tensor_count // KVH)
    rows = bias_ref.shape[0]
    heads_per = HEADS // tensor_count
    groups = len(masks) // per

    load_copies = []
    if weight_masks:
        load_copies = weight_copies(place, weight, weight_out, weight_semaphores, weight_masks)
    for copy in load_copies:
        copy.start()

    @beside_copies(place)
    def _():
        bias = bias_ref[...]
        lane = lax.broadcasted_iota(jnp.int32, (rows, HD), 1)
        for group in range(groups):
            kv_head = (tensor_rank ^ masks[group * per]) // per
            keys, values = [], []
            for piece in pieces:
                halved = piece.shape[1] < KVH * 2 * HD
                start = pl.multiple_of((kv_head // 2 if halved else kv_head) * (2 * HD), 2 * HD)
                keys.append(piece[:, pl.ds(start, HD)])
                values.append(piece[:, pl.ds(pl.multiple_of(start + HD, HD), HD)])
            blocks = []
            for block in queries[group * per : group * per + per]:
                blocks += [block[:, head * HD : (head + 1) * HD] for head in range(heads_per)]
            stacked = jnp.concatenate(blocks, axis=0)
            scores = lax.dot_general(
                stacked,
                jnp.concatenate(keys, axis=0),
                (((1,), (1,)), ((), ())),
                preferred_element_type=jnp.float32,
            )
            weights, totals, level = [], [], []
            for at in range(GROUP):
                shifted = scores[at * rows : (at + 1) * rows] + bias
                row_max = jnp.max(shifted, axis=1, keepdims=True)
                expo = jnp.exp2((shifted - row_max) * FACTOR)
                total = jnp.sum(expo, axis=1, keepdims=True)
                weights.append(expo.astype(jnp.bfloat16))
                totals.append(total)
                level.append(row_max * FACTOR + jnp.log2(total))
            weighted = jnp.dot(
                jnp.concatenate(weights, axis=0),
                jnp.concatenate(values, axis=0),
                preferred_element_type=jnp.float32,
            )
            for low in range(per):
                out = parts[group * per + low]
                levels = jnp.zeros((rows, HD), jnp.float32)
                for head in range(heads_per):
                    at = low * heads_per + head
                    attended = weighted[at * rows : (at + 1) * rows] / totals[at]
                    out[:, head * HD : (head + 1) * HD] = attended.astype(jnp.bfloat16)
                    levels = jnp.where(lane % heads_per == head, level[at], levels)
                out[:, heads_per * HD :] = packed_level(levels, lane, heads_per)

    for copy in load_copies:
        copy.wait()


def combined(parts, heads_per):
    levels = []
    for part in parts:
        level = part[:, heads_per * HD :].astype(jnp.float32)
        levels.append(
            level
            + pltpu.roll(level, HD - heads_per, 1)
            + pltpu.roll(level, HD - 2 * heads_per, 1)
        )
    top = functools.reduce(jnp.maximum, levels)
    shares = [jnp.exp2(level - top) for level in levels]
    total = sum(shares[1:], shares[0])
    shares = [share / total for share in shares]
    heads = []
    for head in range(heads_per):
        terms = [
            share[:, head : head + 1] * part[:, head * HD : (head + 1) * HD].astype(jnp.float32)
            for share, part in zip(shares, parts)
        ]
        heads.append(sum(terms[1:], terms[0]).astype(jnp.bfloat16))
    return jnp.concatenate(heads, axis=1)


def project(rows, weights, found, out):
    for at, (array, block) in enumerate(found):
        product = jnp.dot(rows, weights[array][block], preferred_element_type=jnp.float32)
        out[at] = product.astype(out.dtype)


def project_away_kernel(heads_per, part_count, found, weight_masks, place, *refs):
    parts, refs = refs[:part_count], refs[part_count:]
    load_copies = []
    if weight_masks:
        *refs, weight_out, weight_semaphores = refs
        weight, refs = refs[0], refs[1:]
        load_copies = weight_copies(place, weight, weight_out, weight_semaphores, weight_masks)
    *weights, out, attended = refs
    for copy in load_copies:
        copy.start()

    @beside_copies(place)
    def _():
        rows = combined(parts, heads_per)
        attended[...] = rows
        project(rows, weights, found, out)

    for copy in load_copies:
        copy.wait()


def project_home_kernel(found, attended, *refs):
    project(attended[...], refs[:-1], found, refs[-1])


def add_far_kernel(home, sibling, *outputs):
    for at, out in enumerate(outputs):
        out[...] = (home[at] + sibling[at].astype(jnp.float32)).astype(out.dtype)


def project_near_kernel(found, first, attended, sibling, after, *refs):
    weights, outputs = refs[: len(refs) - len(found)], refs[len(refs) - len(found) :]
    rows = attended[...]
    for at, (array, block) in enumerate(found):
        product = jnp.dot(rows, weights[array][block], preferred_element_type=jnp.float32)
        total = product + sibling[first + at].astype(jnp.float32)
        outputs[at][...] = total.astype(outputs[at].dtype)


def add_own_kernel(own, *refs):
    total = own[...]
    for received in refs[:-1]:
        total = total + received[...].astype(jnp.float32)
    refs[-1][...] = total


def local(hidden_in, queries, new_kv, kv_pages, out_weight, move_pages, page_table, lengths):
    tensor_count = lax.axis_size("tensor")
    inst_count = lax.axis_size("inst")
    section_rank = lax.axis_index("section")
    per = max(1, tensor_count // KVH)
    heads_per = HEADS // tensor_count
    requests, slots = page_table.shape
    rows = requests * STEPS
    own_pages = kv_pages[0]
    pages, page_tokens, width = own_pages.shape
    capacity = move_pages.shape[2]
    moves = in_hbm(move_pages.reshape(-1))
    depth, features = out_weight.shape[1:]
    chunk = features // tensor_count
    half = tensor_count // 2
    vmem = pl.BlockSpec(memory_space=pltpu.VMEM)
    hbm = pl.BlockSpec(memory_space=pltpu.HBM)
    peers = [mask for mask in range(tensor_count) if mask & per == 0]

    if len(peers) == 4:
        peers = [0, 6, 4, 2]
    far = half // 2
    home_masks = list(range(2, tensor_count, 2))
    if half == 4:
        home_masks = [6, 4, 2]
    home_masks.insert(far, 0)
    away_masks = [mask ^ 1 for mask in home_masks]
    unit = tensor_count // 8
    loads, filled = [], 0
    for share in LOAD_SHARES:
        loads.append((away_masks + home_masks)[filled : filled + share * unit])
        filled += share * unit
    moved_weights = []

    def weight_parts(wanted):
        arrays = [
            (masks, array) for masks, array in zip(loads, moved_weights) if set(masks) & set(wanted)
        ]
        found = [
            (at, masks.index(mask))
            for mask in wanted
            for at, (masks, _) in enumerate(arrays)
            if mask in masks
        ]
        return [array for _, array in arrays], found

    weight = in_hbm(out_weight)

    def weight_shape(count):
        return pltpu.VMEM((count, depth, chunk), jnp.bfloat16)

    smem = pl.BlockSpec(memory_space=pltpu.SMEM)
    place = pl.pallas_call(
        place_kernel,
        out_shape=pltpu.SMEM((2,), jnp.int32),
        out_specs=smem,
        name="place",
    )()

    own_queries = queries[0]
    all_queries = {mask: swapped(own_queries, mask) for mask in peers[1:]}
    own_flat = own_pages.reshape(pages * page_tokens, width)
    partner_flat = swapped(own_flat, per)
    *leaving, moved = pl.pallas_call(
        functools.partial(pick_kernel, capacity, loads[0]),
        out_shape=[jax.ShapeDtypeStruct((capacity, page_tokens, width // 2), jnp.bfloat16)]
        * (2 * (inst_count - 1))
        + [weight_shape(len(loads[0]))],
        in_specs=[smem] + [hbm] * 3,
        out_specs=[vmem] * (2 * inst_count - 1),
        scratch_shapes=[
            pltpu.SMEM(moves.shape, jnp.int32),
            pltpu.SemaphoreType.DMA,
            pltpu.SemaphoreType.DMA(((inst_count - 1) * capacity * KVH,)),
            pltpu.SemaphoreType.DMA((len(loads[0]),)),
        ],
        compiler_params=pltpu.CompilerParams(vmem_limit_bytes=2 * MEGA),
        name="pick",
    )(place, moves, in_hbm(own_pages), weight)
    moved_weights.append(moved)
    arrived = []
    for shift in range(1, inst_count):
        for other in range(2):
            pairs = [
                (
                    inst * tensor_count + rank,
                    (inst + shift) % inst_count * tensor_count + (rank ^ (per * other)),
                )
                for inst in range(inst_count)
                for rank in range(tensor_count)
            ]
            sent = leaving[2 * (shift - 1) + other].reshape(capacity * page_tokens, width // 2)
            arrived.append(lax.ppermute(sent, ("inst", "tensor"), pairs))
    if page_tokens * capacity % 16:
        arrived = [jnp.concatenate(arrived, axis=0)]
    owned = [own_queries, own_flat, new_kv[0]]
    columns = 2 * own_flat.shape[0] + sum(piece.shape[0] for piece in arrived) + rows

    bias, all_queries[0], own_tokens, new_tokens, moved = pl.pallas_call(
        functools.partial(
            prepare_kernel, (pages, page_tokens, capacity), loads[1]
        ),
        out_shape=[jax.ShapeDtypeStruct((rows, columns), jnp.float32)]
        + [pltpu.VMEM(value.shape, value.dtype) for value in owned]
        + [weight_shape(len(loads[1]))],
        in_specs=[smem] + [hbm] * 7 + [vmem],
        out_specs=[vmem] * 5,
        scratch_shapes=[
            pltpu.SMEM((slots, requests), jnp.int32),
            pltpu.SMEM((requests,), jnp.int32),
            pltpu.SMEM(moves.shape, jnp.int32),
            pltpu.SemaphoreType.DMA((6,)),
            pltpu.SemaphoreType.DMA((len(loads[1]),)),
        ],
        compiler_params=pltpu.CompilerParams(vmem_limit_bytes=2 * MEGA),
        name="prepare",
    )(
        place,
        in_hbm(page_table.T),
        in_hbm(lengths),
        moves,
        weight,
        *[in_hbm(value) for value in owned],
        all_queries[peers[per]],
    )
    moved_weights.append(moved)
    pieces = [own_tokens, partner_flat, *arrived, new_tokens]

    part_shape = jax.ShapeDtypeStruct((rows, heads_per * HD + HD), jnp.bfloat16)

    def attend(masks, weight_masks, *after):
        loading = bool(weight_masks)
        results = pl.pallas_call(
            functools.partial(attend_kernel, masks, weight_masks, len(pieces), len(after)),
            out_shape=[part_shape] * len(masks) + [weight_shape(len(weight_masks))] * loading,
            in_specs=[smem] + [vmem] * (1 + len(masks) + len(pieces) + len(after)) + [hbm] * loading,
            out_specs=[vmem] * (len(masks) + loading),
            scratch_shapes=[pltpu.SemaphoreType.DMA((len(weight_masks),))] * loading,
            compiler_params=pltpu.CompilerParams(vmem_limit_bytes=8 * MEGA),
            name="attend",
        )(place, bias, *[all_queries[mask] for mask in masks], *pieces, *after, *[weight] * loading)
        moved_weights.append(results[-1] if loading else None)
        return dict(zip(masks, results))

    received, after = {}, []
    for masks, weight_masks in (
        (peers[per : 2 * per], loads[2]),
        (peers[2 * per :], loads[3]),
        (peers[:per], loads[4]),
    ):
        parts = attend(masks, weight_masks, *after)
        after = [received[peers[per]] if received else parts[masks[0]]]
        received.update({mask: swapped(part, mask) for mask, part in parts.items() if mask})
    received = [parts[0]] + [received[mask] for mask in peers[1:]]

    project_params = pltpu.CompilerParams(vmem_limit_bytes=4 * MEGA)
    loading = bool(loads[5])
    away_weights, found = weight_parts(away_masks)
    away, attended, *moved = pl.pallas_call(
        functools.partial(project_away_kernel, heads_per, half, found, loads[5]),
        in_specs=[smem] + [vmem] * half + [hbm] * loading + [vmem] * len(away_weights),
        out_specs=[vmem] * (2 + loading),
        out_shape=[
            jax.ShapeDtypeStruct((half, rows, chunk), jnp.bfloat16),
            jax.ShapeDtypeStruct((rows, depth), jnp.bfloat16),
        ]
        + [weight_shape(len(loads[5]))] * loading,
        scratch_shapes=[pltpu.SemaphoreType.DMA((len(loads[5]),))] * loading,
        compiler_params=project_params,
        name="project_away",
    )(place, *received, *[weight] * loading, *away_weights)
    moved_weights.extend(moved)
    sibling = swapped(away, 1)
    home_weights, found = weight_parts(home_masks[:far])
    home = pl.pallas_call(
        functools.partial(project_home_kernel, found),
        in_specs=[vmem] * (1 + len(home_weights)),
        out_specs=vmem,
        out_shape=jax.ShapeDtypeStruct((far, rows, chunk), jnp.float32),
        compiler_params=project_params,
        name="project_far",
    )(attended, *home_weights)
    add_params = pltpu.CompilerParams(vmem_limit_bytes=2 * MEGA)
    own_shape = jax.ShapeDtypeStruct((rows, chunk), jnp.float32)
    sum_shape = jax.ShapeDtypeStruct((rows, chunk), jnp.bfloat16)
    far_sums = pl.pallas_call(
        add_far_kernel,
        in_specs=[vmem] * 2,
        out_specs=[vmem] * far,
        out_shape=[sum_shape] * far,
        compiler_params=add_params,
        name="add_far",
    )(home, sibling)
    home_weights, found = weight_parts(home_masks[far + 1 :])
    near_sums = pl.pallas_call(
        functools.partial(project_near_kernel, found, far + 1),
        in_specs=[vmem] * (3 + len(home_weights)),
        out_specs=[vmem] * len(found),
        out_shape=[sum_shape] * len(found),
        compiler_params=project_params,
        name="project_near",
    )(attended, sibling, far_sums[0], *home_weights)
    home_weights, found = weight_parts(home_masks[far : far + 1])
    (own,) = pl.pallas_call(
        functools.partial(project_near_kernel, found, far),
        in_specs=[vmem] * (3 + len(home_weights)),
        out_specs=[vmem],
        out_shape=[own_shape],
        compiler_params=project_params,
        name="project_own",
    )(attended, sibling, near_sums[0], *home_weights)
    received = [swapped(total, mask) for mask, total in zip(home_masks, far_sums)]
    projected = pl.pallas_call(
        add_own_kernel,
        in_specs=[vmem] * (1 + far),
        out_specs=vmem,
        out_shape=own_shape,
        compiler_params=add_params,
        name="add_own",
    )(own, *received)
    for mask, total in zip(home_masks[far + 1 :], near_sums):
        projected = projected + swapped(total, mask).astype(jnp.float32)
    after_first = (hidden_in.astype(jnp.float32) + projected).astype(jnp.bfloat16)
    handed_over = lax.ppermute(after_first, "section", [(0, 1), (1, 0)])
    after_second = (handed_over.astype(jnp.float32) + projected).astype(jnp.bfloat16)
    result = jnp.where(section_rank == 0, after_first, after_second)
    return result[None]


def solution(mesh):
    return jax.shard_map(
        local,
        mesh=mesh,
        in_specs=(
            P("inst", "tensor"),
            P("section", "inst", "tensor"),
            P("section", "inst", None),
            P("section", "inst", "tensor", None),
            P("section", "tensor", None),
            P("inst", None, None),
            P("inst", None),
            P("inst"),
        ),
        out_specs=P("section", "inst", "tensor"),
        check_vma=False,
    )
```

```python
import functools
import math

import jax
import jax.numpy as jnp
from jax import lax
from jax.experimental import pallas as pl
from jax.experimental.pallas import tpu as pltpu
from jax.sharding import PartitionSpec as P

HEADS = 64
KVH = 8
HD = 128
STEPS = 4
GROUP = HEADS // KVH
MASKED = -1e30
LOG2E = 1.4426950408889634
FACTOR = LOG2E / math.sqrt(HD)
MEGA = 1024 * 1024
LOAD_SHARES = (1, 1, 0, 1, 4, 1)


def swapped(value, mask):
    count = lax.axis_size("tensor")
    return lax.ppermute(value, "tensor", [(source, source ^ mask) for source in range(count)])


def in_hbm(value):
    return pltpu.with_memory_space_constraint(value, pltpu.HBM)


def place_kernel(place):
    place[0] = lax.axis_index("tensor")
    place[1] = lax.axis_index("inst")


def beside_copies(place):
    return pl.when(place[0] >= 0)


def weight_copies(place, weight, out, semaphores, masks):
    rank = place[0]
    chunk = out.shape[2]
    copies = []
    for at, mask in enumerate(masks):
        start = pl.multiple_of((rank ^ mask) * chunk, chunk)
        copies.append(
            pltpu.make_async_copy(
                weight.at[0, :, pl.ds(start, chunk)], out.at[at], semaphores.at[at]
            )
        )
    return copies


def pick_kernel(capacity, weight_masks, place, moves_hbm, pages, weight, *refs):
    outputs, refs = refs[:-5], refs[-5:]
    weight_out, moves, moves_semaphore, semaphores, weight_semaphores = refs
    moves_copy = pltpu.make_async_copy(moves_hbm, moves, moves_semaphore)
    load_copies = weight_copies(place, weight, weight_out, weight_semaphores, weight_masks)
    for copy in [moves_copy] + load_copies:
        copy.start()
    moves_copy.wait()
    tensor_count, inst_count = lax.axis_size("tensor"), lax.axis_size("inst")
    per = max(1, tensor_count // KVH)
    side = place[0] // per % 2
    copies = []
    for shift in range(1, inst_count):
        target = place[1] + shift
        target = jnp.where(target >= inst_count, target - inst_count, target)
        for slot in range(capacity):
            page = moves[target * capacity + slot]
            for other in range(2):
                out = outputs[2 * (shift - 1) + other]
                for pair in range(KVH // 2):
                    head = 2 * pair + (side if other == 0 else 1 - side)
                    start = pl.multiple_of(head * (2 * HD), 2 * HD)
                    copies.append(
                        pltpu.make_async_copy(
                            pages.at[page, :, pl.ds(start, 2 * HD)],
                            out.at[slot, :, 2 * HD * pair : 2 * HD * (pair + 1)],
                            semaphores.at[len(copies)],
                        )
                    )
    for copy in copies:
        copy.start()
    for copy in copies + load_copies:
        copy.wait()


def packed_level(level, lane, heads_per):
    top = level.astype(jnp.bfloat16).astype(jnp.float32)
    rest = level - top
    middle = rest.astype(jnp.bfloat16).astype(jnp.float32)
    level = jnp.where(lane < heads_per, top, jnp.where(lane < 2 * heads_per, middle, rest - middle))
    return level.astype(jnp.bfloat16)


def prepare_kernel(shape, weight_masks, place, table_hbm, lengths_hbm, moves_hbm, weight, *refs):
    owned, refs = refs[:3], refs[4:]
    bias_out, owned_out, refs = refs[0], refs[1:4], refs[4:]
    weight_out, table, lengths, moves, semaphores, weight_semaphores = refs
    pages, page_tokens, capacity = shape
    tensor_count, inst_count = lax.axis_size("tensor"), lax.axis_size("inst")
    tensor_rank, inst_rank = place[0], place[1]
    per = max(1, tensor_count // KVH)
    partner = tensor_rank ^ per
    rows, columns = bias_out.shape
    slots, requests = table.shape
    page_size = page_tokens * tensor_count
    copies = [
        pltpu.make_async_copy(source, target, semaphores.at[at])
        for at, (source, target) in enumerate(
            ((table_hbm, table), (lengths_hbm, lengths), (moves_hbm, moves))
        )
    ]
    load_copies = [
        pltpu.make_async_copy(source, target, semaphores.at[3 + at])
        for at, (source, target) in enumerate(zip(owned, owned_out))
    ] + weight_copies(place, weight, weight_out, weight_semaphores, weight_masks)
    for copy in copies + load_copies:
        copy.start()
    for copy in copies:
        copy.wait()

    @beside_copies(place)
    def _():
        row = lax.broadcasted_iota(jnp.int32, (rows, 1), 0)
        row_request, row_step = row // STEPS, row % STEPS
        row_length = jnp.zeros((rows, 1), jnp.int32)
        row_pages = [jnp.zeros((rows, 1), jnp.int32) for _ in range(slots)]
        for request in range(requests):
            here = row_request == request
            row_length = jnp.where(here, lengths[request], row_length)
            for slot in range(slots):
                page = table[slot, request]
                arrived = page - pages
                for own in range(capacity):
                    page = jnp.where(
                        arrived == inst_rank * capacity + own, moves[inst_rank * capacity + own], page
                    )
                row_pages[slot] = jnp.where(here, page, row_pages[slot])

        column = lax.broadcasted_iota(jnp.int32, (1, columns), 1)
        own_columns = pages * page_tokens
        block_columns = capacity * page_tokens
        moved = column - 2 * own_columns
        block = moved // block_columns
        source = inst_rank - block // 2 - 1
        source = jnp.where(source < 0, source + inst_count, source)
        resident = moved < 0
        page = jnp.where(
            resident,
            column % own_columns // page_tokens,
            pages + source * capacity + moved // page_tokens % capacity,
        )
        side = jnp.where(resident, column // own_columns, block % 2)
        token = jnp.where(side == 0, tensor_rank, partner) * page_tokens + column % page_tokens
        use = jnp.zeros((rows, columns), jnp.float32)
        for slot in range(slots):
            live = (row_pages[slot] == page) & (token + slot * page_size < row_length)
            use = use + jnp.where(live, 1.0, 0.0)
        fresh = column - (columns - rows)
        fresh_live = (fresh // STEPS == row_request) & (fresh % STEPS <= row_step)
        fresh_live = fresh_live & ((tensor_rank == 0) | (tensor_rank == per))
        use = jnp.where(fresh >= 0, jnp.where(fresh_live, 1.0, 0.0), use)
        bias_out[...] = jnp.where(use > 0.0, jnp.log2(jnp.maximum(use, 1.0)) / FACTOR, MASKED)

    for copy in load_copies:
        copy.wait()


def attend_kernel(masks, weight_masks, piece_count, after_count, *refs):
    place, bias_ref, refs = refs[0], refs[1], refs[2:]
    tensor_count, tensor_rank = lax.axis_size("tensor"), place[0]
    queries, refs = refs[: len(masks)], refs[len(masks) :]
    pieces, refs = refs[:piece_count], refs[piece_count + after_count :]
    if weight_masks:
        weight, *refs, weight_out, weight_semaphores = refs
    parts = refs
    per = max(1, tensor_count // KVH)
    rows = bias_ref.shape[0]
    heads_per = HEADS // tensor_count
    groups = len(masks) // per

    load_copies = []
    if weight_masks:
        load_copies = weight_copies(place, weight, weight_out, weight_semaphores, weight_masks)
    for at, copy in enumerate(load_copies):
        copy.start(priority=at % 2)

    @beside_copies(place)
    def _():
        bias = bias_ref[...]
        lane = lax.broadcasted_iota(jnp.int32, (rows, HD), 1)
        for group in range(groups):
            kv_head = (tensor_rank ^ masks[group * per]) // per
            keys, values = [], []
            for piece in pieces:
                halved = piece.shape[1] < KVH * 2 * HD
                start = pl.multiple_of((kv_head // 2 if halved else kv_head) * (2 * HD), 2 * HD)
                keys.append(piece[:, pl.ds(start, HD)])
                values.append(piece[:, pl.ds(pl.multiple_of(start + HD, HD), HD)])
            blocks = []
            for block in queries[group * per : group * per + per]:
                blocks += [block[:, head * HD : (head + 1) * HD] for head in range(heads_per)]
            stacked = jnp.concatenate(blocks, axis=0)
            scores = lax.dot_general(
                stacked,
                jnp.concatenate(keys, axis=0),
                (((1,), (1,)), ((), ())),
                preferred_element_type=jnp.float32,
            )
            weights, totals, level = [], [], []
            for at in range(GROUP):
                shifted = scores[at * rows : (at + 1) * rows] + bias
                row_max = jnp.max(shifted, axis=1, keepdims=True)
                expo = jnp.exp2((shifted - row_max) * FACTOR)
                total = jnp.sum(expo, axis=1, keepdims=True)
                weights.append(expo.astype(jnp.bfloat16))
                totals.append(total)
                level.append(row_max * FACTOR + jnp.log2(total))
            weighted = jnp.dot(
                jnp.concatenate(weights, axis=0),
                jnp.concatenate(values, axis=0),
                preferred_element_type=jnp.float32,
            )
            for low in range(per):
                out = parts[group * per + low]
                levels = jnp.zeros((rows, HD), jnp.float32)
                for head in range(heads_per):
                    at = low * heads_per + head
                    attended = weighted[at * rows : (at + 1) * rows] / totals[at]
                    out[:, head * HD : (head + 1) * HD] = attended.astype(jnp.bfloat16)
                    levels = jnp.where(lane % heads_per == head, level[at], levels)
                out[:, heads_per * HD :] = packed_level(levels, lane, heads_per)

    for copy in load_copies:
        copy.wait()


def combined(parts, heads_per):
    levels = []
    for part in parts:
        level = part[:, heads_per * HD :].astype(jnp.float32)
        levels.append(
            level
            + pltpu.roll(level, HD - heads_per, 1)
            + pltpu.roll(level, HD - 2 * heads_per, 1)
        )
    top = functools.reduce(jnp.maximum, levels)
    shares = [jnp.exp2(level - top) for level in levels]
    total = sum(shares[1:], shares[0])
    shares = [share / total for share in shares]
    heads = []
    for head in range(heads_per):
        terms = [
            share[:, head : head + 1] * part[:, head * HD : (head + 1) * HD].astype(jnp.float32)
            for share, part in zip(shares, parts)
        ]
        heads.append(sum(terms[1:], terms[0]).astype(jnp.bfloat16))
    return jnp.concatenate(heads, axis=1)


def project(rows, weights, found, out):
    for at, (array, block) in enumerate(found):
        product = jnp.dot(rows, weights[array][block], preferred_element_type=jnp.float32)
        out[at] = product.astype(out.dtype)


def project_away_kernel(heads_per, part_count, found, weight_masks, place, *refs):
    parts, refs = refs[:part_count], refs[part_count:]
    load_copies = []
    if weight_masks:
        *refs, weight_out, weight_semaphores = refs
        weight, refs = refs[0], refs[1:]
        load_copies = weight_copies(place, weight, weight_out, weight_semaphores, weight_masks)
    *weights, out, attended = refs
    for at, copy in enumerate(load_copies):
        copy.start(priority=at % 2)

    @beside_copies(place)
    def _():
        rows = combined(parts, heads_per)
        attended[...] = rows
        project(rows, weights, found, out)

    for copy in load_copies:
        copy.wait()


def project_home_kernel(found, attended, *refs):
    project(attended[...], refs[:-1], found, refs[-1])


def add_far_kernel(home, sibling, *outputs):
    for at, out in enumerate(outputs):
        out[...] = (home[at] + sibling[at].astype(jnp.float32)).astype(out.dtype)


def project_near_kernel(found, first, attended, sibling, after, *refs):
    weights, outputs = refs[: len(refs) - len(found)], refs[len(refs) - len(found) :]
    rows = attended[...]
    for at, (array, block) in enumerate(found):
        product = jnp.dot(rows, weights[array][block], preferred_element_type=jnp.float32)
        total = product + sibling[first + at].astype(jnp.float32)
        outputs[at][...] = total.astype(outputs[at].dtype)


def add_own_kernel(own, *refs):
    total = own[...]
    for received in refs[:-1]:
        total = total + received[...].astype(jnp.float32)
    refs[-1][...] = total


def local(hidden_in, queries, new_kv, kv_pages, out_weight, move_pages, page_table, lengths):
    tensor_count = lax.axis_size("tensor")
    inst_count = lax.axis_size("inst")
    section_rank = lax.axis_index("section")
    per = max(1, tensor_count // KVH)
    heads_per = HEADS // tensor_count
    requests, slots = page_table.shape
    rows = requests * STEPS
    own_pages = kv_pages[0]
    pages, page_tokens, width = own_pages.shape
    capacity = move_pages.shape[2]
    moves = in_hbm(move_pages.reshape(-1))
    depth, features = out_weight.shape[1:]
    chunk = features // tensor_count
    half = tensor_count // 2
    vmem = pl.BlockSpec(memory_space=pltpu.VMEM)
    hbm = pl.BlockSpec(memory_space=pltpu.HBM)
    peers = [mask for mask in range(tensor_count) if mask & per == 0]

    if len(peers) == 4:
        peers = [0, 6, 4, 2]
    far = half // 2
    home_masks = list(range(2, tensor_count, 2))
    if half == 4:
        home_masks = [6, 4, 2]
    home_masks.insert(far, 0)
    away_masks = [mask ^ 1 for mask in home_masks]
    unit = tensor_count // 8
    loads, filled = [], 0
    for share in LOAD_SHARES:
        loads.append((away_masks + home_masks)[filled : filled + share * unit])
        filled += share * unit
    moved_weights = []

    def weight_parts(wanted):
        arrays = [
            (masks, array) for masks, array in zip(loads, moved_weights) if set(masks) & set(wanted)
        ]
        found = [
            (at, masks.index(mask))
            for mask in wanted
            for at, (masks, _) in enumerate(arrays)
            if mask in masks
        ]
        return [array for _, array in arrays], found

    weight = in_hbm(out_weight)

    def weight_shape(count):
        return pltpu.VMEM((count, depth, chunk), jnp.bfloat16)

    smem = pl.BlockSpec(memory_space=pltpu.SMEM)
    place = pl.pallas_call(
        place_kernel,
        out_shape=pltpu.SMEM((2,), jnp.int32),
        out_specs=smem,
        name="place",
    )()

    own_queries = queries[0]
    all_queries = {mask: swapped(own_queries, mask) for mask in peers[1:]}
    own_flat = own_pages.reshape(pages * page_tokens, width)
    partner_flat = swapped(own_flat, per)
    *leaving, moved = pl.pallas_call(
        functools.partial(pick_kernel, capacity, loads[0]),
        out_shape=[jax.ShapeDtypeStruct((capacity, page_tokens, width // 2), jnp.bfloat16)]
        * (2 * (inst_count - 1))
        + [weight_shape(len(loads[0]))],
        in_specs=[smem] + [hbm] * 3,
        out_specs=[vmem] * (2 * inst_count - 1),
        scratch_shapes=[
            pltpu.SMEM(moves.shape, jnp.int32),
            pltpu.SemaphoreType.DMA,
            pltpu.SemaphoreType.DMA(((inst_count - 1) * capacity * KVH,)),
            pltpu.SemaphoreType.DMA((len(loads[0]),)),
        ],
        compiler_params=pltpu.CompilerParams(vmem_limit_bytes=2 * MEGA),
        name="pick",
    )(place, moves, in_hbm(own_pages), weight)
    moved_weights.append(moved)
    arrived = []
    for shift in range(1, inst_count):
        for other in range(2):
            pairs = [
                (
                    inst * tensor_count + rank,
                    (inst + shift) % inst_count * tensor_count + (rank ^ (per * other)),
                )
                for inst in range(inst_count)
                for rank in range(tensor_count)
            ]
            sent = leaving[2 * (shift - 1) + other].reshape(capacity * page_tokens, width // 2)
            arrived.append(lax.ppermute(sent, ("inst", "tensor"), pairs))
    if page_tokens * capacity % 16:
        arrived = [jnp.concatenate(arrived, axis=0)]
    owned = [own_queries, own_flat, new_kv[0]]
    columns = 2 * own_flat.shape[0] + sum(piece.shape[0] for piece in arrived) + rows

    bias, all_queries[0], own_tokens, new_tokens, moved = pl.pallas_call(
        functools.partial(
            prepare_kernel, (pages, page_tokens, capacity), loads[1]
        ),
        out_shape=[jax.ShapeDtypeStruct((rows, columns), jnp.float32)]
        + [pltpu.VMEM(value.shape, value.dtype) for value in owned]
        + [weight_shape(len(loads[1]))],
        in_specs=[smem] + [hbm] * 7 + [vmem],
        out_specs=[vmem] * 5,
        scratch_shapes=[
            pltpu.SMEM((slots, requests), jnp.int32),
            pltpu.SMEM((requests,), jnp.int32),
            pltpu.SMEM(moves.shape, jnp.int32),
            pltpu.SemaphoreType.DMA((6,)),
            pltpu.SemaphoreType.DMA((len(loads[1]),)),
        ],
        compiler_params=pltpu.CompilerParams(vmem_limit_bytes=2 * MEGA),
        name="prepare",
    )(
        place,
        in_hbm(page_table.T),
        in_hbm(lengths),
        moves,
        weight,
        *[in_hbm(value) for value in owned],
        all_queries[peers[per]],
    )
    moved_weights.append(moved)
    pieces = [own_tokens, partner_flat, *arrived, new_tokens]

    part_shape = jax.ShapeDtypeStruct((rows, heads_per * HD + HD), jnp.bfloat16)

    def attend(masks, weight_masks, *after):
        loading = bool(weight_masks)
        results = pl.pallas_call(
            functools.partial(attend_kernel, masks, weight_masks, len(pieces), len(after)),
            out_shape=[part_shape] * len(masks) + [weight_shape(len(weight_masks))] * loading,
            in_specs=[smem] + [vmem] * (1 + len(masks) + len(pieces) + len(after)) + [hbm] * loading,
            out_specs=[vmem] * (len(masks) + loading),
            scratch_shapes=[pltpu.SemaphoreType.DMA((len(weight_masks),))] * loading,
            compiler_params=pltpu.CompilerParams(vmem_limit_bytes=8 * MEGA),
            name="attend",
        )(place, bias, *[all_queries[mask] for mask in masks], *pieces, *after, *[weight] * loading)
        moved_weights.append(results[-1] if loading else None)
        return dict(zip(masks, results))

    received, after = {}, []
    for masks, weight_masks in (
        (peers[per : 2 * per], loads[2]),
        (peers[2 * per :], loads[3]),
        (peers[:per], loads[4]),
    ):
        parts = attend(masks, weight_masks, *after)
        after = [received[peers[per]] if received else parts[masks[0]]]
        received.update({mask: swapped(part, mask) for mask, part in parts.items() if mask})
    received = [parts[0]] + [received[mask] for mask in peers[1:]]

    project_params = pltpu.CompilerParams(vmem_limit_bytes=4 * MEGA)
    loading = bool(loads[5])
    away_weights, found = weight_parts(away_masks)
    away, attended, *moved = pl.pallas_call(
        functools.partial(project_away_kernel, heads_per, half, found, loads[5]),
        in_specs=[smem] + [vmem] * half + [hbm] * loading + [vmem] * len(away_weights),
        out_specs=[vmem] * (2 + loading),
        out_shape=[
            jax.ShapeDtypeStruct((half, rows, chunk), jnp.bfloat16),
            jax.ShapeDtypeStruct((rows, depth), jnp.bfloat16),
        ]
        + [weight_shape(len(loads[5]))] * loading,
        scratch_shapes=[pltpu.SemaphoreType.DMA((len(loads[5]),))] * loading,
        compiler_params=project_params,
        name="project_away",
    )(place, *received, *[weight] * loading, *away_weights)
    moved_weights.extend(moved)
    sibling = swapped(away, 1)
    home_weights, found = weight_parts(home_masks[:far])
    home = pl.pallas_call(
        functools.partial(project_home_kernel, found),
        in_specs=[vmem] * (1 + len(home_weights)),
        out_specs=vmem,
        out_shape=jax.ShapeDtypeStruct((far, rows, chunk), jnp.float32),
        compiler_params=project_params,
        name="project_far",
    )(attended, *home_weights)
    add_params = pltpu.CompilerParams(vmem_limit_bytes=2 * MEGA)
    own_shape = jax.ShapeDtypeStruct((rows, chunk), jnp.float32)
    sum_shape = jax.ShapeDtypeStruct((rows, chunk), jnp.bfloat16)
    far_sums = pl.pallas_call(
        add_far_kernel,
        in_specs=[vmem] * 2,
        out_specs=[vmem] * far,
        out_shape=[sum_shape] * far,
        compiler_params=add_params,
        name="add_far",
    )(home, sibling)
    home_weights, found = weight_parts(home_masks[far + 1 :])
    near_sums = pl.pallas_call(
        functools.partial(project_near_kernel, found, far + 1),
        in_specs=[vmem] * (3 + len(home_weights)),
        out_specs=[vmem] * len(found),
        out_shape=[sum_shape] * len(found),
        compiler_params=project_params,
        name="project_near",
    )(attended, sibling, far_sums[0], *home_weights)
    home_weights, found = weight_parts(home_masks[far : far + 1])
    (own,) = pl.pallas_call(
        functools.partial(project_near_kernel, found, far),
        in_specs=[vmem] * (3 + len(home_weights)),
        out_specs=[vmem],
        out_shape=[own_shape],
        compiler_params=project_params,
        name="project_own",
    )(attended, sibling, near_sums[0], *home_weights)
    received = [swapped(total, mask) for mask, total in zip(home_masks, far_sums)]
    projected = pl.pallas_call(
        add_own_kernel,
        in_specs=[vmem] * (1 + far),
        out_specs=vmem,
        out_shape=own_shape,
        compiler_params=add_params,
        name="add_own",
    )(own, *received)
    for mask, total in zip(home_masks[far + 1 :], near_sums):
        projected = projected + swapped(total, mask).astype(jnp.float32)
    after_first = (hidden_in.astype(jnp.float32) + projected).astype(jnp.bfloat16)
    handed_over = lax.ppermute(after_first, "section", [(0, 1), (1, 0)])
    after_second = (handed_over.astype(jnp.float32) + projected).astype(jnp.bfloat16)
    result = jnp.where(section_rank == 0, after_first, after_second)
    return result[None]


def solution(mesh):
    return jax.shard_map(
        local,
        mesh=mesh,
        in_specs=(
            P("inst", "tensor"),
            P("section", "inst", "tensor"),
            P("section", "inst", None),
            P("section", "inst", "tensor", None),
            P("section", "tensor", None),
            P("inst", None, None),
            P("inst", None),
            P("inst"),
        ),
        out_specs=P("section", "inst", "tensor"),
        check_vma=False,
    )
```

```python
import functools
import math

import jax
import jax.numpy as jnp
from jax import lax
from jax.experimental import pallas as pl
from jax.experimental.pallas import tpu as pltpu
from jax.sharding import PartitionSpec as P

HEADS = 64
KVH = 8
HD = 128
STEPS = 4
GROUP = HEADS // KVH
MASKED = -1e30
LOG2E = 1.4426950408889634
FACTOR = LOG2E / math.sqrt(HD)
MEGA = 1024 * 1024
LOAD_SHARES = (1, 1, 0, 1, 4, 1)


def swapped(value, mask):
    count = lax.axis_size("tensor")
    return lax.ppermute(value, "tensor", [(source, source ^ mask) for source in range(count)])


def in_hbm(value):
    return pltpu.with_memory_space_constraint(value, pltpu.HBM)


def place_kernel(place):
    place[0] = lax.axis_index("tensor")
    place[1] = lax.axis_index("inst")


def beside_copies(place):
    return pl.when(place[0] >= 0)


def weight_copies(place, weight, out, semaphores, masks):
    rank = place[0]
    chunk = out.shape[2]
    copies = []
    for at, mask in enumerate(masks):
        start = pl.multiple_of((rank ^ mask) * chunk, chunk)
        copies.append(
            pltpu.make_async_copy(
                weight.at[0, :, pl.ds(start, chunk)], out.at[at], semaphores.at[at]
            )
        )
    return copies


def pick_kernel(capacity, weight_masks, place, moves_hbm, pages, weight, *refs):
    outputs, refs = refs[:-5], refs[-5:]
    weight_out, moves, moves_semaphore, semaphores, weight_semaphores = refs
    moves_copy = pltpu.make_async_copy(moves_hbm, moves, moves_semaphore)
    load_copies = weight_copies(place, weight, weight_out, weight_semaphores, weight_masks)
    for copy in [moves_copy] + load_copies:
        copy.start()
    moves_copy.wait()
    tensor_count, inst_count = lax.axis_size("tensor"), lax.axis_size("inst")
    per = max(1, tensor_count // KVH)
    side = place[0] // per % 2
    copies = []
    for shift in range(1, inst_count):
        target = place[1] + shift
        target = jnp.where(target >= inst_count, target - inst_count, target)
        for slot in range(capacity):
            page = moves[target * capacity + slot]
            for other in range(2):
                out = outputs[2 * (shift - 1) + other]
                for pair in range(KVH // 2):
                    head = 2 * pair + (side if other == 0 else 1 - side)
                    start = pl.multiple_of(head * (2 * HD), 2 * HD)
                    copies.append(
                        pltpu.make_async_copy(
                            pages.at[page, :, pl.ds(start, 2 * HD)],
                            out.at[slot, :, 2 * HD * pair : 2 * HD * (pair + 1)],
                            semaphores.at[len(copies)],
                        )
                    )
    for copy in copies:
        copy.start()
    for copy in copies + load_copies:
        copy.wait()


def packed_level(level, lane, heads_per):
    top = level.astype(jnp.bfloat16).astype(jnp.float32)
    rest = level - top
    middle = rest.astype(jnp.bfloat16).astype(jnp.float32)
    level = jnp.where(lane < heads_per, top, jnp.where(lane < 2 * heads_per, middle, rest - middle))
    return level.astype(jnp.bfloat16)


def prepare_kernel(shape, weight_masks, place, table_hbm, lengths_hbm, moves_hbm, weight, *refs):
    owned, refs = refs[:3], refs[4:]
    bias_out, owned_out, refs = refs[0], refs[1:4], refs[4:]
    weight_out, table, lengths, moves, semaphores, weight_semaphores = refs
    pages, page_tokens, capacity = shape
    tensor_count, inst_count = lax.axis_size("tensor"), lax.axis_size("inst")
    tensor_rank, inst_rank = place[0], place[1]
    per = max(1, tensor_count // KVH)
    partner = tensor_rank ^ per
    rows, columns = bias_out.shape
    slots, requests = table.shape
    page_size = page_tokens * tensor_count
    copies = [
        pltpu.make_async_copy(source, target, semaphores.at[at])
        for at, (source, target) in enumerate(
            ((table_hbm, table), (lengths_hbm, lengths), (moves_hbm, moves))
        )
    ]
    load_copies = [
        pltpu.make_async_copy(source, target, semaphores.at[3 + at])
        for at, (source, target) in enumerate(zip(owned, owned_out))
    ] + weight_copies(place, weight, weight_out, weight_semaphores, weight_masks)
    for copy in copies + load_copies:
        copy.start()
    for copy in copies:
        copy.wait()

    @beside_copies(place)
    def _():
        row = lax.broadcasted_iota(jnp.int32, (rows, 1), 0)
        row_request, row_step = row // STEPS, row % STEPS
        row_length = jnp.zeros((rows, 1), jnp.int32)
        row_pages = [jnp.zeros((rows, 1), jnp.int32) for _ in range(slots)]
        for request in range(requests):
            here = row_request == request
            row_length = jnp.where(here, lengths[request], row_length)
            for slot in range(slots):
                page = table[slot, request]
                arrived = page - pages
                for own in range(capacity):
                    page = jnp.where(
                        arrived == inst_rank * capacity + own, moves[inst_rank * capacity + own], page
                    )
                row_pages[slot] = jnp.where(here, page, row_pages[slot])

        column = lax.broadcasted_iota(jnp.int32, (1, columns), 1)
        own_columns = pages * page_tokens
        block_columns = capacity * page_tokens
        moved = column - 2 * own_columns
        block = moved // block_columns
        source = inst_rank - block // 2 - 1
        source = jnp.where(source < 0, source + inst_count, source)
        resident = moved < 0
        page = jnp.where(
            resident,
            column % own_columns // page_tokens,
            pages + source * capacity + moved // page_tokens % capacity,
        )
        side = jnp.where(resident, column // own_columns, block % 2)
        token = jnp.where(side == 0, tensor_rank, partner) * page_tokens + column % page_tokens
        use = jnp.zeros((rows, columns), jnp.float32)
        for slot in range(slots):
            live = (row_pages[slot] == page) & (token + slot * page_size < row_length)
            use = use + jnp.where(live, 1.0, 0.0)
        fresh = column - (columns - rows)
        fresh_live = (fresh // STEPS == row_request) & (fresh % STEPS <= row_step)
        fresh_live = fresh_live & ((tensor_rank == 0) | (tensor_rank == per))
        use = jnp.where(fresh >= 0, jnp.where(fresh_live, 1.0, 0.0), use)
        bias_out[...] = jnp.where(use > 0.0, jnp.log2(jnp.maximum(use, 1.0)) / FACTOR, MASKED)

    for copy in load_copies:
        copy.wait()


def attend_kernel(masks, weight_masks, piece_count, after_count, *refs):
    place, bias_ref, refs = refs[0], refs[1], refs[2:]
    tensor_count, tensor_rank = lax.axis_size("tensor"), place[0]
    queries, refs = refs[: len(masks)], refs[len(masks) :]
    pieces, refs = refs[:piece_count], refs[piece_count + after_count :]
    if weight_masks:
        weight, *refs, weight_out, weight_semaphores = refs
    parts = refs
    per = max(1, tensor_count // KVH)
    rows = bias_ref.shape[0]
    heads_per = HEADS // tensor_count
    groups = len(masks) // per

    load_copies = []
    if weight_masks:
        load_copies = weight_copies(place, weight, weight_out, weight_semaphores, weight_masks)
    for copy in load_copies:
        copy.start()

    @beside_copies(place)
    def _():
        bias = bias_ref[...]
        lane = lax.broadcasted_iota(jnp.int32, (rows, HD), 1)
        for group in range(groups):
            kv_head = (tensor_rank ^ masks[group * per]) // per
            keys, values = [], []
            for piece in pieces:
                halved = piece.shape[1] < KVH * 2 * HD
                start = pl.multiple_of((kv_head // 2 if halved else kv_head) * (2 * HD), 2 * HD)
                keys.append(piece[:, pl.ds(start, HD)])
                values.append(piece[:, pl.ds(pl.multiple_of(start + HD, HD), HD)])
            blocks = []
            for block in queries[group * per : group * per + per]:
                blocks += [block[:, head * HD : (head + 1) * HD] for head in range(heads_per)]
            stacked = jnp.concatenate(blocks, axis=0)
            scores = lax.dot_general(
                stacked,
                jnp.concatenate(keys, axis=0),
                (((1,), (1,)), ((), ())),
                preferred_element_type=jnp.float32,
            )
            weights, totals, level = [], [], []
            for at in range(GROUP):
                shifted = scores[at * rows : (at + 1) * rows] + bias
                row_max = jnp.max(shifted, axis=1, keepdims=True)
                expo = jnp.exp2((shifted - row_max) * FACTOR)
                total = jnp.sum(expo, axis=1, keepdims=True)
                weights.append(expo.astype(jnp.bfloat16))
                totals.append(total)
                level.append(row_max * FACTOR + jnp.log2(total))
            weighted = jnp.dot(
                jnp.concatenate(weights, axis=0),
                jnp.concatenate(values, axis=0),
                preferred_element_type=jnp.float32,
            )
            for low in range(per):
                out = parts[group * per + low]
                levels = jnp.zeros((rows, HD), jnp.float32)
                for head in range(heads_per):
                    at = low * heads_per + head
                    attended = weighted[at * rows : (at + 1) * rows] / totals[at]
                    out[:, head * HD : (head + 1) * HD] = attended.astype(jnp.bfloat16)
                    levels = jnp.where(lane % heads_per == head, level[at], levels)
                out[:, heads_per * HD :] = packed_level(levels, lane, heads_per)

    for copy in load_copies:
        copy.wait()


def combined(parts, heads_per):
    levels = []
    for part in parts:
        level = part[:, heads_per * HD :].astype(jnp.float32)
        levels.append(
            level
            + pltpu.roll(level, HD - heads_per, 1)
            + pltpu.roll(level, HD - 2 * heads_per, 1)
        )
    top = functools.reduce(jnp.maximum, levels)
    shares = [jnp.exp2(level - top) for level in levels]
    total = sum(shares[1:], shares[0])
    shares = [share / total for share in shares]
    heads = []
    for head in range(heads_per):
        terms = [
            share[:, head : head + 1] * part[:, head * HD : (head + 1) * HD].astype(jnp.float32)
            for share, part in zip(shares, parts)
        ]
        heads.append(sum(terms[1:], terms[0]).astype(jnp.bfloat16))
    return jnp.concatenate(heads, axis=1)


def project(rows, weights, found, out):
    for at, (array, block) in enumerate(found):
        product = jnp.dot(rows, weights[array][block], preferred_element_type=jnp.float32)
        out[at] = product.astype(out.dtype)


def project_away_kernel(heads_per, part_count, found, weight_masks, place, *refs):
    parts, refs = refs[:part_count], refs[part_count:]
    load_copies = []
    if weight_masks:
        *refs, weight_out, weight_semaphores = refs
        weight, refs = refs[0], refs[1:]
        load_copies = weight_copies(place, weight, weight_out, weight_semaphores, weight_masks)
    *weights, out, attended = refs
    for copy in load_copies:
        copy.start()

    @beside_copies(place)
    def _():
        rows = combined(parts, heads_per)
        attended[...] = rows
        project(rows, weights, found, out)

    for copy in load_copies:
        copy.wait()


def project_home_kernel(found, attended, *refs):
    project(attended[...], refs[:-1], found, refs[-1])


def add_far_kernel(home, sibling, *outputs):
    for at, out in enumerate(outputs):
        out[...] = (home[at] + sibling[at].astype(jnp.float32)).astype(out.dtype)


def project_near_kernel(found, first, attended, sibling, after, *refs):
    weights, outputs = refs[: len(refs) - len(found)], refs[len(refs) - len(found) :]
    rows = attended[...]
    for at, (array, block) in enumerate(found):
        product = jnp.dot(rows, weights[array][block], preferred_element_type=jnp.float32)
        total = product + sibling[first + at].astype(jnp.float32)
        outputs[at][...] = total.astype(outputs[at].dtype)


def add_own_kernel(own, *refs):
    total = own[...]
    for received in refs[:-1]:
        total = total + received[...].astype(jnp.float32)
    refs[-1][...] = total


def local(hidden_in, queries, new_kv, kv_pages, out_weight, move_pages, page_table, lengths):
    tensor_count = lax.axis_size("tensor")
    inst_count = lax.axis_size("inst")
    section_rank = lax.axis_index("section")
    per = max(1, tensor_count // KVH)
    heads_per = HEADS // tensor_count
    requests, slots = page_table.shape
    rows = requests * STEPS
    own_pages = kv_pages[0]
    pages, page_tokens, width = own_pages.shape
    capacity = move_pages.shape[2]
    moves = in_hbm(move_pages.reshape(-1))
    depth, features = out_weight.shape[1:]
    chunk = features // tensor_count
    half = tensor_count // 2
    vmem = pl.BlockSpec(memory_space=pltpu.VMEM)
    hbm = pl.BlockSpec(memory_space=pltpu.HBM)
    peers = [mask for mask in range(tensor_count) if mask & per == 0]

    if len(peers) == 4:
        peers = [0, 6, 4, 2]
    far = half // 2
    home_masks = list(range(2, tensor_count, 2))
    if half == 4:
        home_masks = [4, 6, 2]
    home_masks.insert(far, 0)
    away_masks = [mask ^ 1 for mask in home_masks]
    unit = tensor_count // 8
    loads, filled = [], 0
    for share in LOAD_SHARES:
        loads.append((away_masks + home_masks)[filled : filled + share * unit])
        filled += share * unit
    moved_weights = []

    def weight_parts(wanted):
        arrays = [
            (masks, array) for masks, array in zip(loads, moved_weights) if set(masks) & set(wanted)
        ]
        found = [
            (at, masks.index(mask))
            for mask in wanted
            for at, (masks, _) in enumerate(arrays)
            if mask in masks
        ]
        return [array for _, array in arrays], found

    weight = in_hbm(out_weight)

    def weight_shape(count):
        return pltpu.VMEM((count, depth, chunk), jnp.bfloat16)

    smem = pl.BlockSpec(memory_space=pltpu.SMEM)
    place = pl.pallas_call(
        place_kernel,
        out_shape=pltpu.SMEM((2,), jnp.int32),
        out_specs=smem,
        name="place",
    )()

    own_queries = queries[0]
    all_queries = {mask: swapped(own_queries, mask) for mask in peers[1:]}
    own_flat = own_pages.reshape(pages * page_tokens, width)
    partner_flat = swapped(own_flat, per)
    *leaving, moved = pl.pallas_call(
        functools.partial(pick_kernel, capacity, loads[0]),
        out_shape=[jax.ShapeDtypeStruct((capacity, page_tokens, width // 2), jnp.bfloat16)]
        * (2 * (inst_count - 1))
        + [weight_shape(len(loads[0]))],
        in_specs=[smem] + [hbm] * 3,
        out_specs=[vmem] * (2 * inst_count - 1),
        scratch_shapes=[
            pltpu.SMEM(moves.shape, jnp.int32),
            pltpu.SemaphoreType.DMA,
            pltpu.SemaphoreType.DMA(((inst_count - 1) * capacity * KVH,)),
            pltpu.SemaphoreType.DMA((len(loads[0]),)),
        ],
        compiler_params=pltpu.CompilerParams(vmem_limit_bytes=2 * MEGA),
        name="pick",
    )(place, moves, in_hbm(own_pages), weight)
    moved_weights.append(moved)
    arrived = []
    for shift in range(1, inst_count):
        for other in range(2):
            pairs = [
                (
                    inst * tensor_count + rank,
                    (inst + shift) % inst_count * tensor_count + (rank ^ (per * other)),
                )
                for inst in range(inst_count)
                for rank in range(tensor_count)
            ]
            sent = leaving[2 * (shift - 1) + other].reshape(capacity * page_tokens, width // 2)
            arrived.append(lax.ppermute(sent, ("inst", "tensor"), pairs))
    if page_tokens * capacity % 16:
        arrived = [jnp.concatenate(arrived, axis=0)]
    owned = [own_queries, own_flat, new_kv[0]]
    columns = 2 * own_flat.shape[0] + sum(piece.shape[0] for piece in arrived) + rows

    bias, all_queries[0], own_tokens, new_tokens, moved = pl.pallas_call(
        functools.partial(
            prepare_kernel, (pages, page_tokens, capacity), loads[1]
        ),
        out_shape=[jax.ShapeDtypeStruct((rows, columns), jnp.float32)]
        + [pltpu.VMEM(value.shape, value.dtype) for value in owned]
        + [weight_shape(len(loads[1]))],
        in_specs=[smem] + [hbm] * 7 + [vmem],
        out_specs=[vmem] * 5,
        scratch_shapes=[
            pltpu.SMEM((slots, requests), jnp.int32),
            pltpu.SMEM((requests,), jnp.int32),
            pltpu.SMEM(moves.shape, jnp.int32),
            pltpu.SemaphoreType.DMA((6,)),
            pltpu.SemaphoreType.DMA((len(loads[1]),)),
        ],
        compiler_params=pltpu.CompilerParams(vmem_limit_bytes=2 * MEGA),
        name="prepare",
    )(
        place,
        in_hbm(page_table.T),
        in_hbm(lengths),
        moves,
        weight,
        *[in_hbm(value) for value in owned],
        all_queries[peers[per]],
    )
    moved_weights.append(moved)
    pieces = [own_tokens, partner_flat, *arrived, new_tokens]

    part_shape = jax.ShapeDtypeStruct((rows, heads_per * HD + HD), jnp.bfloat16)

    def attend(masks, weight_masks, *after):
        loading = bool(weight_masks)
        results = pl.pallas_call(
            functools.partial(attend_kernel, masks, weight_masks, len(pieces), len(after)),
            out_shape=[part_shape] * len(masks) + [weight_shape(len(weight_masks))] * loading,
            in_specs=[smem] + [vmem] * (1 + len(masks) + len(pieces) + len(after)) + [hbm] * loading,
            out_specs=[vmem] * (len(masks) + loading),
            scratch_shapes=[pltpu.SemaphoreType.DMA((len(weight_masks),))] * loading,
            compiler_params=pltpu.CompilerParams(vmem_limit_bytes=8 * MEGA),
            name="attend",
        )(place, bias, *[all_queries[mask] for mask in masks], *pieces, *after, *[weight] * loading)
        moved_weights.append(results[-1] if loading else None)
        return dict(zip(masks, results))

    received, after = {}, []
    for masks, weight_masks in (
        (peers[per : 2 * per], loads[2]),
        (peers[2 * per :], loads[3]),
        (peers[:per], loads[4]),
    ):
        parts = attend(masks, weight_masks, *after)
        after = [received[peers[per]] if received else parts[masks[0]]]
        received.update({mask: swapped(part, mask) for mask, part in parts.items() if mask})
    received = [parts[0]] + [received[mask] for mask in peers[1:]]

    project_params = pltpu.CompilerParams(vmem_limit_bytes=4 * MEGA)
    loading = bool(loads[5])
    away_weights, found = weight_parts(away_masks)
    away, attended, *moved = pl.pallas_call(
        functools.partial(project_away_kernel, heads_per, half, found, loads[5]),
        in_specs=[smem] + [vmem] * half + [hbm] * loading + [vmem] * len(away_weights),
        out_specs=[vmem] * (2 + loading),
        out_shape=[
            jax.ShapeDtypeStruct((half, rows, chunk), jnp.bfloat16),
            jax.ShapeDtypeStruct((rows, depth), jnp.bfloat16),
        ]
        + [weight_shape(len(loads[5]))] * loading,
        scratch_shapes=[pltpu.SemaphoreType.DMA((len(loads[5]),))] * loading,
        compiler_params=project_params,
        name="project_away",
    )(place, *received, *[weight] * loading, *away_weights)
    moved_weights.extend(moved)
    sibling = swapped(away, 1)
    home_weights, found = weight_parts(home_masks[:far])
    home = pl.pallas_call(
        functools.partial(project_home_kernel, found),
        in_specs=[vmem] * (1 + len(home_weights)),
        out_specs=vmem,
        out_shape=jax.ShapeDtypeStruct((far, rows, chunk), jnp.float32),
        compiler_params=project_params,
        name="project_far",
    )(attended, *home_weights)
    add_params = pltpu.CompilerParams(vmem_limit_bytes=2 * MEGA)
    own_shape = jax.ShapeDtypeStruct((rows, chunk), jnp.float32)
    sum_shape = jax.ShapeDtypeStruct((rows, chunk), jnp.bfloat16)
    far_sums = pl.pallas_call(
        add_far_kernel,
        in_specs=[vmem] * 2,
        out_specs=[vmem] * far,
        out_shape=[sum_shape] * far,
        compiler_params=add_params,
        name="add_far",
    )(home, sibling)
    home_weights, found = weight_parts(home_masks[far + 1 :])
    near_sums = pl.pallas_call(
        functools.partial(project_near_kernel, found, far + 1),
        in_specs=[vmem] * (3 + len(home_weights)),
        out_specs=[vmem] * len(found),
        out_shape=[sum_shape] * len(found),
        compiler_params=project_params,
        name="project_near",
    )(attended, sibling, far_sums[0], *home_weights)
    home_weights, found = weight_parts(home_masks[far : far + 1])
    (own,) = pl.pallas_call(
        functools.partial(project_near_kernel, found, far),
        in_specs=[vmem] * (3 + len(home_weights)),
        out_specs=[vmem],
        out_shape=[own_shape],
        compiler_params=project_params,
        name="project_own",
    )(attended, sibling, near_sums[0], *home_weights)
    received = [swapped(total, mask) for mask, total in zip(home_masks, far_sums)]
    projected = pl.pallas_call(
        add_own_kernel,
        in_specs=[vmem] * (1 + far),
        out_specs=vmem,
        out_shape=own_shape,
        compiler_params=add_params,
        name="add_own",
    )(own, *received)
    for mask, total in zip(home_masks[far + 1 :], near_sums):
        projected = projected + swapped(total, mask).astype(jnp.float32)
    after_first = (hidden_in.astype(jnp.float32) + projected).astype(jnp.bfloat16)
    handed_over = lax.ppermute(after_first, "section", [(0, 1), (1, 0)])
    after_second = (handed_over.astype(jnp.float32) + projected).astype(jnp.bfloat16)
    result = jnp.where(section_rank == 0, after_first, after_second)
    return result[None]


def solution(mesh):
    return jax.shard_map(
        local,
        mesh=mesh,
        in_specs=(
            P("inst", "tensor"),
            P("section", "inst", "tensor"),
            P("section", "inst", None),
            P("section", "inst", "tensor", None),
            P("section", "tensor", None),
            P("inst", None, None),
            P("inst", None),
            P("inst"),
        ),
        out_specs=P("section", "inst", "tensor"),
        check_vma=False,
    )
```
